32 devices in a mesh: snap: 16 (over z, y, x), span: 2 (over core).
Axes of the slice: x: 2, y: 2, z: 4, core: 2. Of those that a mesh axis runs over, the one named last changes fastest.
Arguments:
- features: bfloat16 [2, 32, 512, 512], P('span', 'snap'), may hold values from -6 to 6
- block_values: bfloat16 [2, 32, 4, 4, 128, 128], P('span', 'snap'), may hold values from -0.25 to 0.25
- block_cols: int32 [2, 32, 4, 4], P('span', 'snap'), may hold values from 0 to 3, as said below
- block_counts: int32 [2, 32, 4], P('span', 'snap'), may hold values from 1 to 4, as said below
- band_coeffs: int32 [2, 32, 32], P('span'), may hold values from 1 to 8
- graph_layer_weight: bfloat16 [2, 512, 512], replicated, may hold values from -0.25 to 0.25
- up_weight: bfloat16 [2, 512, 1024], replicated, may hold values from -0.25 to 0.25
- down_weight: bfloat16 [2, 1024, 512], replicated, may hold values from -0.1875 to 0.1875
Outputs:
- vertex_features: bfloat16 [2, 32, 512, 512], P('span', None, 'snap')
The draws below stay inside these ranges and needn't reach their ends.
Inputs may be any that keep to these rules, and one draw needn't show every extreme that they name: `block_cols`: the block columns named in one block row are distinct, and the first is the row's own block; only the first block_counts entries of a row are used. `block_counts`: block row 0 of every snapshot uses all 4 blocks.
All inputs are finite; a program needn't handle non-finite values.
Results may differ from the reference program's by a relative error of at most 0.018.
Values may be sent and summed in bfloat16 or wider, within the bound.
No kernel may reach another device: no remote copies, remote signals or barrier semaphores. Data moves between devices by JAX's collectives and lax.ppermute only.
A program may use at most 128 MiB of HBM per device.

```python
import jax
import jax.numpy as jnp
from jax import lax

D = 512
HID = 1024
BLK = 128
KMAX = 4
BAND = 32
LAYERS = 2
SPANS = 2
TC = 32
V = 512
NB = 4


def draw_block_cols(key, part):
    scores = jax.random.randint(key, (SPANS, TC, NB, NB), 0, 1 << 20) * NB + jnp.arange(NB)
    diagonal = jnp.arange(NB)[:, None] == jnp.arange(NB)[None, :]
    scores = jnp.where(diagonal, -1, scores)
    ordered = jnp.argsort(scores, axis=-1, stable=True)
    return ordered[..., :KMAX].astype(jnp.int32)


def draw_block_counts(key, part):
    counts = jax.random.randint(key, (SPANS, TC, NB), 1, KMAX + 1)
    counts = counts.at[:, :, 0].set(KMAX)
    return counts.astype(jnp.int32)


def set_ends(array, own_key, least, largest):
    spot = [jax.random.randint(jax.random.fold_in(own_key, axis), (), 0, length) for axis, length in enumerate(array.shape)]
    main_axis = array.shape.index(max(array.shape))
    neighbour = spot[:main_axis] + [(spot[main_axis] + 1) % array.shape[main_axis]] + spot[main_axis + 1:]
    return array.at[tuple(spot)].set(least).at[tuple(neighbour)].set(largest)


def level_of(stream_key, dims, pieces, least, top_value):
    def one(axis_at, parts):
        steps = jax.random.uniform(jax.random.fold_in(jax.random.fold_in(stream_key, 6), axis_at), (parts,), jnp.float32, least / len(pieces), top_value / len(pieces))
        return jnp.repeat(jnp.exp(steps), dims[axis_at] // parts).reshape((-1,) + (1,) * (len(dims) - axis_at - 1))

    factor_of = one(*pieces[0])
    for cut in pieces[1:]:
        factor_of = factor_of * one(*cut)
    return factor_of


def scatter_about(stream_key, shape, deviation, bound, shards=(), held_as=jnp.bfloat16):
    gain = level_of(stream_key, shape, shards, -0.22, 0.18) if shards else 1.0
    array = jax.random.normal(stream_key, shape, jnp.float32) * deviation * gain
    return jnp.minimum(jnp.maximum(array, -bound), bound).astype(held_as)


def setup_inputs(seed: int = 0) -> dict:
    arg_keys = jax.random.split(jax.random.key(seed), 9)
    features = scatter_about(arg_keys[0], (SPANS, TC, V, D), 1.0, 6.0, ((0, 2), (1, 16)))
    block_values = scatter_about(arg_keys[1], (SPANS, TC, NB, KMAX, BLK, BLK), (BLK * KMAX) ** -0.5, 0.25, ((0, 2), (1, 16)))
    block_cols = draw_block_cols(jax.random.fold_in(arg_keys[8], 71), 0)
    block_counts = draw_block_counts(jax.random.fold_in(arg_keys[8], 71), 0)
    band_coeffs = set_ends(jax.random.randint(arg_keys[4], (SPANS, TC, BAND), 1, 9), jax.random.fold_in(arg_keys[4], 1), 1, 8).astype(jnp.int32)
    graph_layer_weight = scatter_about(arg_keys[5], (LAYERS, D, D), D ** -0.5, 0.25)
    up_weight = scatter_about(arg_keys[6], (LAYERS, D, HID), D ** -0.5, 0.25)
    down_weight = scatter_about(arg_keys[7], (LAYERS, HID, D), HID ** -0.5, 0.1875)
    return {"features": features, "block_values": block_values, "block_cols": block_cols, "block_counts": block_counts, "band_coeffs": band_coeffs, "graph_layer_weight": graph_layer_weight, "up_weight": up_weight, "down_weight": down_weight}


def make_band(band_coeffs):
    frames_all = SPANS * TC
    coeffs = band_coeffs.reshape(frames_all, BAND).astype(jnp.float32)
    positions = jnp.arange(frames_all)
    lag_offsets = jnp.arange(BAND)
    valid_lags = (positions[:, None] - lag_offsets[None, :] >= 0).astype(jnp.float32)
    scaled = coeffs * valid_lags
    diagonal_weight_strip = scaled / lax.optimization_barrier(jnp.sum(scaled, axis=1, keepdims=True))
    rounded = lax.optimization_barrier(diagonal_weight_strip.astype(jnp.bfloat16))
    return rounded.astype(jnp.float32)

def sparse_frame(frame_rows, frame_values, frame_cols, frame_counts):
    blocks = frame_rows.reshape(NB, BLK, D)
    selected_entries = blocks[frame_cols]
    live_slots = jnp.arange(KMAX)[None, :] < frame_counts[:, None]
    retained_values = jnp.where(live_slots[:, :, None, None], frame_values, jnp.zeros((), frame_values.dtype))
    lag_total_sum = jnp.einsum('qmtp,qmps->qts', retained_values.astype(jnp.float32), selected_entries.astype(jnp.float32))
    return lag_total_sum.reshape(V, D).astype(jnp.bfloat16)

def reference(features, block_values, block_cols, block_counts, band_coeffs, graph_layer_weight, up_weight, down_weight):
    frames_all = SPANS * TC
    current = features.reshape(frames_all, V, D)
    values_all = block_values.reshape(frames_all, NB, KMAX, BLK, BLK)
    cols_all = block_cols.reshape(frames_all, NB, KMAX)
    counts_all = block_counts.reshape(frames_all, NB)
    diagonal_weight_strip = make_band(band_coeffs)
    for layer_index in range(LAYERS):

        def frame_step(items):
            frame_rows, frame_values, frame_cols, frame_counts = items
            weighted = jnp.dot(frame_rows, graph_layer_weight[layer_index], preferred_element_type=jnp.float32).astype(jnp.bfloat16)
            return sparse_frame(weighted, frame_values, frame_cols, frame_counts)
        propagated = lax.map(frame_step, (current, values_all, cols_all, counts_all))
        grouped = jnp.moveaxis(propagated.reshape(frames_all, NB, BLK, D), 1, 0)

        def vertex_step(block_rows):
            padded = jnp.concatenate([jnp.zeros((BAND - 1, BLK, D), jnp.bfloat16), block_rows], axis=0)
            mixed = jnp.zeros((frames_all, BLK, D), jnp.float32)
            for lag_value in range(BAND):
                start = BAND - 1 - lag_value
                mixed = mixed + diagonal_weight_strip[:, lag_value][:, None, None] * padded[start:start + frames_all].astype(jnp.float32)
            mean_square = lax.optimization_barrier(jnp.mean(mixed * mixed, axis=-1, keepdims=True))
            normed = (mixed * lax.rsqrt(mean_square + 1e-06)).astype(jnp.bfloat16)
            flat_rows = normed.reshape(frames_all * BLK, D)
            activated = jax.nn.relu(jnp.dot(flat_rows, up_weight[layer_index], preferred_element_type=jnp.float32)).astype(jnp.bfloat16)
            branch = jnp.dot(activated, down_weight[layer_index], preferred_element_type=jnp.float32)
            return (mixed + branch.reshape(frames_all, BLK, D)).astype(jnp.bfloat16)
        outputs = lax.map(vertex_step, grouped)
        current = jnp.moveaxis(outputs, 0, 1).reshape(frames_all, V, D)
    return current.reshape(SPANS, TC, V, D)
```

```python
import functools

import jax
import jax.numpy as jnp
from jax import lax
from jax.experimental import pallas as pl
from jax.experimental.pallas import tpu as pltpu
from jax.sharding import PartitionSpec as P

BAND = 32
LAYERS = 2
TILE = 256
REACH = 3
ROWS = 512
EVERY = ("snap", "span")
MIB = 1 << 20


def dot(left, right):
    return jnp.dot(left, right, preferred_element_type=jnp.float32)


def in_vmem(shape, dtype=jnp.bfloat16):
    return pltpu.VMEM(shape, dtype)


def vmem_specs(count):
    return [pl.BlockSpec(memory_space=pltpu.VMEM)] * count


def held(array):
    return pltpu.with_memory_space_constraint(array, pltpu.VMEM)


def in_hbm(array):
    return pltpu.with_memory_space_constraint(array, pltpu.HBM)


def hbm_specs(count):
    return [pl.BlockSpec(memory_space=pltpu.HBM)] * count


def params(mib=16):
    return pltpu.CompilerParams(vmem_limit_bytes=mib * MIB)


def propagate(frame, values_ref, cols_ref, counts_ref, weighted_ref, dense_ref, sent_ref):
    block_rows, slots, size, _ = values_ref.shape[1:]
    group = dense_ref.shape[0] // size
    own = sent_ref.shape[2]
    width = sent_ref.shape[3]
    for first in range(0, block_rows, group):
        dense_ref[...] = jnp.zeros_like(dense_ref)
        for row in range(group):
            for slot in range(slots):

                @pl.when(slot < counts_ref[frame, first + row])
                def place():
                    column = pl.multiple_of(cols_ref[frame, first + row, slot] * size, size)
                    dense_ref[pl.ds(row * size, size), pl.ds(column, size)] = values_ref[
                        frame, first + row, slot
                    ]

        summed = dot(dense_ref[...], weighted_ref[...]).astype(jnp.bfloat16)
        owners = group * size // own
        sent_ref[pl.ds(first * size // own, owners), frame] = summed.reshape(owners, own, width)


def copies(pairs, sems):
    return [pltpu.make_async_copy(*pair, sems.at[place]) for place, pair in enumerate(pairs)]


def first_kernel(
    features_ref,
    weight_ref,
    values_ref,
    cols_ref,
    counts_ref,
    sent_ref,
    features_in,
    weight_in,
    values_in,
    cols_in,
    counts_in,
    weighted_ref,
    dense_ref,
    sems,
):
    frames = range(features_in.shape[0])
    loads = copies(
        [(weight_ref.at[0], weight_in)]
        + [(features_ref.at[0, frame], features_in.at[frame]) for frame in frames]
        + [(cols_ref.at[0], cols_in), (counts_ref.at[0], counts_in)]
        + [(values_ref.at[0, frame], values_in.at[frame]) for frame in frames],
        sems,
    )
    for load in loads:
        load.start()
    loads[0].wait()
    for frame in frames:
        loads[1 + frame].wait()
        weighted_ref[...] = dot(features_in[frame], weight_in[...]).astype(jnp.bfloat16)
        if frame == 0:
            loads[1 + len(frames)].wait()
            loads[2 + len(frames)].wait()
        loads[3 + len(frames) + frame].wait()
        propagate(frame, values_in, cols_in, counts_in, weighted_ref, dense_ref, sent_ref)


def later_kernel(
    arrived_ref, values_ref, cols_ref, counts_ref, sent_ref, weighted_ref, dense_ref
):
    for frame in range(arrived_ref.shape[1]):
        weighted_ref[...] = arrived_ref[:, frame].reshape(weighted_ref.shape)
        propagate(frame, values_ref, cols_ref, counts_ref, weighted_ref, dense_ref, sent_ref)


def graph_scratch(values, width):
    block_rows, _, size, _ = values.shape[-4:]
    vertices = block_rows * size
    return [
        pltpu.VMEM((vertices, width), jnp.bfloat16),
        pltpu.VMEM((min(block_rows, 4) * size, vertices), jnp.bfloat16),
    ]


def first_graph(features, weight, values, cols, counts, owners):
    frames, vertices, width = features.shape[1:]
    return pl.pallas_call(
        first_kernel,
        name="first_graph",
        out_shape=in_vmem((owners, frames, vertices // owners, width)),
        in_specs=hbm_specs(5),
        out_specs=pl.BlockSpec(memory_space=pltpu.VMEM),
        scratch_shapes=[
            pltpu.VMEM(features.shape[1:], jnp.bfloat16),
            pltpu.VMEM(weight.shape[1:], jnp.bfloat16),
            pltpu.VMEM(values.shape[1:], jnp.bfloat16),
            pltpu.SMEM(cols.shape[1:], jnp.int32),
            pltpu.SMEM(counts.shape[1:], jnp.int32),
            *graph_scratch(values, width),
            pltpu.SemaphoreType.DMA((3 + 2 * frames,)),
        ],
        compiler_params=params(32),
    )(*map(in_hbm, (features, weight, values, cols, counts)))


def later_graph(arrived, values, cols, counts):
    smem = pl.BlockSpec(memory_space=pltpu.SMEM)
    return pl.pallas_call(
        later_kernel,
        name="later_graph",
        out_shape=in_vmem(arrived.shape),
        in_specs=vmem_specs(2) + [smem, smem],
        out_specs=pl.BlockSpec(memory_space=pltpu.VMEM),
        scratch_shapes=graph_scratch(values, arrived.shape[-1]),
        compiler_params=params(),
    )(held(arrived), held(values), cols, counts)


def band_weights(coeffs, frames_in_tile):
    frames = coeffs.shape[0]
    back = (REACH - 1) * frames_in_tile
    lags = jnp.arange(BAND)
    valid = jnp.arange(frames)[:, None] - lags[None, :] >= 0
    scaled = jnp.where(valid, coeffs.astype(jnp.float32), 0.0)
    weights = scaled / jnp.sum(scaled, axis=1, keepdims=True)
    lag = back + (jnp.arange(frames) % frames_in_tile)[:, None] - jnp.arange(
        REACH * frames_in_tile
    )
    chosen = jnp.where(lag[:, :, None] == lags, weights[:, None, :], 0.0)
    return jnp.sum(chosen, axis=-1).astype(jnp.bfloat16)


def spread_kernel(own, weights_ref, tiles_ref):
    tiles, reach, rows, _ = tiles_ref.shape
    in_tile = rows // own
    spread = (
        lax.broadcasted_iota(jnp.int32, (rows, in_tile), 0) // own
        == lax.broadcasted_iota(jnp.int32, (rows, in_tile), 1)
    ).astype(jnp.bfloat16)
    same = (
        lax.broadcasted_iota(jnp.int32, (rows, rows), 0) % own
        == lax.broadcasted_iota(jnp.int32, (rows, rows), 1) % own
    )
    for tile in range(tiles):
        down = dot(spread, weights_ref[pl.ds(tile * in_tile, in_tile)]).astype(jnp.bfloat16)
        for source in range(reach):
            part = down[:, source * in_tile : (source + 1) * in_tile]
            across = lax.dot_general(
                part, spread, (((1,), (1,)), ((), ())), preferred_element_type=jnp.float32
            )
            tiles_ref[tile, source] = jnp.where(same, across, 0.0).astype(jnp.bfloat16)


def spread_band(weights, own):
    tiles = weights.shape[0] * own // TILE
    return pl.pallas_call(
        functools.partial(spread_kernel, own),
        name="spread_band",
        out_shape=jax.ShapeDtypeStruct((tiles, REACH, TILE, TILE), jnp.bfloat16),
        in_specs=vmem_specs(1),
        out_specs=pl.BlockSpec(memory_space=pltpu.VMEM),
        compiler_params=params(),
    )(weights)


def rows_of(ref, tile, steps):
    in_span = ref.shape[0] // steps
    first = (tile % in_span) * steps
    return (pl.ds(first, steps), tile // in_span)


def mix(place, band_tile, sources, mixed_ref, normed_ref):
    total = None
    for part, source in sources:
        term = dot(band_tile[part], source)
        total = term if total is None else total + term
    mean_square = jnp.mean(total * total, axis=-1, keepdims=True)
    rows = pl.ds(place * TILE, TILE)
    mixed_ref[rows] = total
    normed_ref[rows] = (total * lax.rsqrt(mean_square + 1e-06)).astype(jnp.bfloat16)


def perceptron(mixed_ref, normed_ref, up, down):
    active = jnp.maximum(dot(normed_ref[...], up), 0.0).astype(jnp.bfloat16)
    return (mixed_ref[...] + dot(active, down)).astype(jnp.bfloat16)


def middle_kernel(
    layer,
    arrived_ref,
    band_ref,
    up_ref,
    down_ref,
    next_ref,
    sent_ref,
    band_in,
    up_in,
    down_in,
    next_in,
    mixed_ref,
    normed_ref,
    sems,
):
    tiles, steps = band_ref.shape[0], TILE // (arrived_ref.shape[2] * arrived_ref.shape[3])
    width = mixed_ref.shape[1]
    together = ROWS // TILE
    loads = copies(
        [(band_ref.at[tile], band_in.at[tile]) for tile in range(tiles)]
        + [
            (up_ref.at[layer], up_in),
            (down_ref.at[layer], down_in),
            (next_ref.at[layer + 1], next_in),
        ],
        sems,
    )
    order = [*range(together), tiles, tiles + 1, tiles + 2, *range(together, tiles)]
    for place in order:
        loads[place].start()
    for first in range(0, tiles, together):
        for place, tile in enumerate(range(first, first + together)):
            loads[tile].wait()
            sources = [
                (
                    REACH - 1 - back,
                    arrived_ref[rows_of(arrived_ref, tile - back, steps)].reshape(TILE, width),
                )
                for back in range(min(REACH, tile + 1))
            ]
            mix(place, band_in.at[tile], sources, mixed_ref, normed_ref)
        if first == 0:
            loads[tiles].wait()
            loads[tiles + 1].wait()
        layer_out = perceptron(mixed_ref, normed_ref, up_in[...], down_in[...])
        if first == 0:
            loads[tiles + 2].wait()
        result = dot(layer_out, next_in[...]).astype(jnp.bfloat16)
        result = result.reshape(together, steps, *sent_ref.shape[2:])
        for place in range(together):
            sent_ref[rows_of(sent_ref, first + place, steps)] = result[place]


def row_scratch(width):
    return [pltpu.VMEM((ROWS, width), jnp.float32), pltpu.VMEM((ROWS, width), jnp.bfloat16)]


def middle_stage(layer, arrived, band, up, down, following):
    width = up.shape[1]
    return pl.pallas_call(
        functools.partial(middle_kernel, layer),
        name="middle_stage",
        out_shape=in_vmem(arrived.shape),
        in_specs=vmem_specs(1) + hbm_specs(4),
        out_specs=pl.BlockSpec(memory_space=pltpu.VMEM),
        scratch_shapes=[
            pltpu.VMEM(band.shape, jnp.bfloat16),
            *(pltpu.VMEM(array.shape[1:], jnp.bfloat16) for array in (up, down, following)),
            *row_scratch(width),
            pltpu.SemaphoreType.DMA((band.shape[0] + 3,)),
        ],
        compiler_params=params(24),
    )(held(arrived), *map(in_hbm, (band, up, down, following)))


def last_kernel(
    layer, flip, arrived_ref, band_ref, up_ref, down_ref, out_ref, mixed_ref, normed_ref
):
    span = lax.axis_index("span")
    span = 1 - span if flip else span
    steps = TILE // (arrived_ref.shape[2] * arrived_ref.shape[3])
    in_span = arrived_ref.shape[0] // steps
    width = mixed_ref.shape[1]
    own = arrived_ref.shape[3]
    frames = TILE // own
    together = ROWS // TILE
    for first in range(0, in_span, together):
        for place in range(together):
            tile = span * in_span + first + place
            sources = [
                (
                    REACH - 1 - back,
                    arrived_ref[
                        rows_of(arrived_ref, jnp.maximum(tile - back, 0), steps)
                    ].reshape(TILE, width),
                )
                for back in range(REACH)
            ]
            mix(place, band_ref.at[tile], sources, mixed_ref, normed_ref)
        layer_out = perceptron(mixed_ref, normed_ref, up_ref[layer], down_ref[layer])
        out_ref[pl.ds(first * frames, together * frames)] = layer_out.reshape(
            together * frames, own, width
        )


def last_stage(layer, flip, arrived, band, up, down):
    width = up.shape[1]
    owners, _, frames, own, _ = arrived.shape
    return pl.pallas_call(
        functools.partial(last_kernel, layer, flip),
        name="last_stage",
        out_shape=in_vmem((owners * frames, own, width)),
        in_specs=vmem_specs(4),
        out_specs=pl.BlockSpec(memory_space=pltpu.VMEM),
        scratch_shapes=row_scratch(width),
        compiler_params=params(),
    )(held(arrived), held(band), held(up), held(down))


def assemble_kernel(kept_ref, received_ref, out_ref, sems):
    span = lax.axis_index("span")
    loads = copies(
        [(kept_ref, out_ref.at[:, span]), (received_ref, out_ref.at[:, 1 - span])], sems
    )
    for load in loads:
        load.start()
    for load in loads:
        load.wait()


def assemble(kept, received):
    frames, own, width = kept.shape
    return pl.pallas_call(
        assemble_kernel,
        name="assemble",
        out_shape=pltpu.HBM((frames, 2, own, width), jnp.bfloat16),
        in_specs=vmem_specs(2),
        out_specs=hbm_specs(1)[0],
        scratch_shapes=[pltpu.SemaphoreType.DMA((2,))],
        compiler_params=params(),
    )(held(kept), held(received))


def exchange(blocks):
    return lax.all_to_all(blocks, EVERY, split_axis=0, concat_axis=0, tiled=True)


def local(
    features,
    block_values,
    block_cols,
    block_counts,
    band_coeffs,
    graph_layer_weight,
    up_weight,
    down_weight,
):
    snaps, spans = lax.axis_size("snap"), lax.axis_size("span")
    span = lax.axis_index("span")
    swap = [(0, 1), (1, 0)]
    owners = snaps * spans
    frames, vertices, width = features.shape[1:]
    own = vertices // owners
    by_owner = (snaps, spans, frames, own, width)

    sent = first_graph(
        features, graph_layer_weight, block_values, block_cols, block_counts, owners
    )
    other_coeffs = lax.ppermute(band_coeffs[0], "span", swap)
    ordered = jnp.where(
        span == 0,
        jnp.concatenate([band_coeffs[0], other_coeffs]),
        jnp.concatenate([other_coeffs, band_coeffs[0]]),
    )
    band = spread_band(band_weights(ordered, TILE // own), own)
    for layer in range(LAYERS - 1):
        arrived = exchange(sent).reshape(by_owner)
        sent = middle_stage(layer, arrived, band, up_weight, down_weight, graph_layer_weight)
        arrived = exchange(sent.reshape(owners, frames, own, width))
        sent = later_graph(arrived, block_values[0], block_cols[0], block_counts[0])
    arrived = exchange(sent).reshape(by_owner)
    give = last_stage(LAYERS - 1, True, arrived, band, up_weight, down_weight)
    received = lax.ppermute(give, "span", swap)
    kept = last_stage(LAYERS - 1, False, arrived, band, up_weight, down_weight)
    return assemble(kept, received).reshape(1, snaps * frames, spans * own, width)


def solution(mesh):
    in_specs = (
        P("span", "snap", None, None),
        P("span", "snap", None, None, None, None),
        P("span", "snap", None, None),
        P("span", "snap", None),
        P("span", None, None),
        P(),
        P(),
        P(),
    )
    out_specs = P("span", None, "snap", None)
    return jax.shard_map(local, mesh=mesh, in_specs=in_specs, out_specs=out_specs, check_vma=False)
```

```python
import functools

import jax
import jax.numpy as jnp
from jax import lax
from jax.experimental import pallas as pl
from jax.experimental.pallas import tpu as pltpu
from jax.sharding import PartitionSpec as P

BAND = 32
LAYERS = 2
TILE = 256
REACH = 3
ROWS = 512
EVERY = ("snap", "span")
MIB = 1 << 20


def dot(left, right):
    return jnp.dot(left, right, preferred_element_type=jnp.float32)


def in_vmem(shape, dtype=jnp.bfloat16):
    return pltpu.VMEM(shape, dtype)


def vmem_specs(count):
    return [pl.BlockSpec(memory_space=pltpu.VMEM)] * count


def held(array):
    return pltpu.with_memory_space_constraint(array, pltpu.VMEM)


def in_hbm(array):
    return pltpu.with_memory_space_constraint(array, pltpu.HBM)


def hbm_specs(count):
    return [pl.BlockSpec(memory_space=pltpu.HBM)] * count


def params(mib=16):
    return pltpu.CompilerParams(vmem_limit_bytes=mib * MIB)


def copies(pairs, sems):
    return [pltpu.make_async_copy(*pair, sems.at[place]) for place, pair in enumerate(pairs)]


def lay_out(frame, values_ref, cols_ref, counts_ref, dense_ref):
    block_rows, slots, size, _ = values_ref.shape[1:]
    dense_ref[frame] = jnp.zeros(dense_ref.shape[1:], dense_ref.dtype)
    for row in range(block_rows):
        for slot in reversed(range(slots)):
            column = pl.multiple_of(cols_ref[frame, row, slot] * size, size)
            block = values_ref[frame, row, slot]
            used = slot < counts_ref[frame, row]
            dense_ref[frame, pl.ds(row * size, size), pl.ds(column, size)] = jnp.where(
                used, block, jnp.zeros_like(block)
            )


def propagate(frame, dense_ref, weighted, sent_ref):
    vertices = dense_ref.shape[1]
    rows = min(vertices, 512)
    own, width = sent_ref.shape[2:]
    for first in range(0, vertices, rows):
        summed = dot(dense_ref[frame, pl.ds(first, rows)], weighted).astype(jnp.bfloat16)
        sent_ref[pl.ds(first // own, rows // own), frame] = summed.reshape(
            rows // own, own, width
        )


def band_rows(coeffs, first_frame, frames_in_tile, copies_of):
    frames = coeffs.shape[0]
    back = (REACH - 1) * frames_in_tile
    lags = lax.broadcasted_iota(jnp.int32, coeffs.shape, 1)
    here = first_frame + lax.broadcasted_iota(jnp.int32, coeffs.shape, 0)
    scaled = jnp.where(here >= lags, coeffs.astype(jnp.float32), 0.0)
    weights = scaled / jnp.sum(scaled, axis=1, keepdims=True)
    sources = REACH * frames_in_tile
    place = lax.broadcasted_iota(jnp.int32, (frames, sources), 0) % frames_in_tile
    lag = back + place - lax.broadcasted_iota(jnp.int32, (frames, sources), 1)
    chosen = jnp.zeros((frames, sources), jnp.float32)
    for each in range(BAND):
        chosen = jnp.where(lag == each, weights[:, each : each + 1], chosen)
    wide = sources * copies_of
    spread = (
        lax.broadcasted_iota(jnp.int32, (sources, wide), 1) // copies_of
        == lax.broadcasted_iota(jnp.int32, (sources, wide), 0)
    ).astype(jnp.bfloat16)
    return dot(chosen.astype(jnp.bfloat16), spread)


def first_kernel(
    features_ref,
    weight_ref,
    values_ref,
    cols_ref,
    counts_ref,
    coeffs_ref,
    sent_ref,
    dense_ref,
    band_ref,
    features_in,
    weight_in,
    values_in,
    cols_in,
    counts_in,
    coeffs_in,
    sems,
):
    frames, vertices, width = features_in.shape
    loads = copies(
        [
            (coeffs_ref.at[0], coeffs_in),
            (weight_ref.at[0], weight_in),
            (features_ref.at[0], features_in),
            (cols_ref.at[0], cols_in),
            (counts_ref.at[0], counts_in),
            (values_ref.at[0], values_in),
        ],
        sems,
    )
    for load in loads:
        load.start()
    own = sent_ref.shape[2]
    loads[0].wait()
    first_frame = lax.axis_index("span") * coeffs_in.shape[0]
    band_ref[...] = band_rows(coeffs_in[...], first_frame, TILE // own, own)
    for load in loads[1:3]:
        load.wait()
    weighted = dot(features_in[...].reshape(frames * vertices, width), weight_in[...])
    weighted = weighted.astype(jnp.bfloat16).reshape(frames, vertices, width)
    for load in loads[3:]:
        load.wait()
    for frame in range(frames):
        lay_out(frame, values_in, cols_in, counts_in, dense_ref)
    for frame in range(frames):
        propagate(frame, dense_ref, weighted[frame], sent_ref)


def later_kernel(arrived_ref, dense_ref, sent_ref):
    _, frames, own, width = arrived_ref.shape
    for frame in range(frames):
        weighted = arrived_ref[:, frame].reshape(dense_ref.shape[1], width)
        propagate(frame, dense_ref, weighted, sent_ref)


def first_graph(features, weight, values, cols, counts, coeffs, owners):
    frames, vertices, width = features.shape[1:]
    own = vertices // owners
    return pl.pallas_call(
        first_kernel,
        name="first_graph",
        out_shape=[
            in_vmem((owners, frames, own, width)),
            in_vmem((frames, vertices, vertices)),
            in_vmem((coeffs.shape[1], REACH * TILE), jnp.float32),
        ],
        in_specs=hbm_specs(6),
        out_specs=vmem_specs(3),
        scratch_shapes=[
            pltpu.VMEM(features.shape[1:], jnp.bfloat16),
            pltpu.VMEM(weight.shape[1:], jnp.bfloat16),
            pltpu.VMEM(values.shape[1:], jnp.bfloat16),
            pltpu.SMEM(cols.shape[1:], jnp.int32),
            pltpu.SMEM(counts.shape[1:], jnp.int32),
            pltpu.VMEM(coeffs.shape[1:], jnp.int32),
            pltpu.SemaphoreType.DMA((6,)),
        ],
        compiler_params=params(20),
    )(*map(in_hbm, (features, weight, values, cols, counts, coeffs)))


def later_graph(arrived, dense):
    return pl.pallas_call(
        later_kernel,
        name="later_graph",
        out_shape=in_vmem(arrived.shape),
        in_specs=vmem_specs(2),
        out_specs=vmem_specs(1)[0],
        compiler_params=params(),
    )(held(arrived), held(dense))


def rows_of(ref, tile, steps):
    in_span = ref.shape[0] // steps
    first = (tile % in_span) * steps
    return (pl.ds(first, steps), tile // in_span)


def mix(place, band_tile, sources, mixed_ref, normed_ref):
    total = None
    for part, source in sources:
        term = dot(band_tile[part], source)
        total = term if total is None else total + term
    mean_square = jnp.mean(total * total, axis=-1, keepdims=True)
    rows = pl.ds(place * TILE, TILE)
    mixed_ref[rows] = total
    normed_ref[rows] = (total * lax.rsqrt(mean_square + 1e-06)).astype(jnp.bfloat16)


def perceptron(mixed_ref, normed_ref, up, down):
    active = jnp.maximum(dot(normed_ref[...], up), 0.0).astype(jnp.bfloat16)
    return (mixed_ref[...] + dot(active, down)).astype(jnp.bfloat16)


def band_tile(rows, own):
    frames, wide = rows.shape
    full = jnp.broadcast_to(rows[:, None, :], (frames, own, wide)).reshape(frames * own, wide)
    same = (
        lax.broadcasted_iota(jnp.int32, full.shape, 0) % own
        == lax.broadcasted_iota(jnp.int32, full.shape, 1) % own
    )
    return jnp.where(same, full, 0.0).astype(jnp.bfloat16)


def weight_rows(tile, in_span, mine_ref, other_ref):
    in_tile = mine_ref.shape[0] // in_span
    rows = pl.ds(tile % in_span * in_tile, in_tile)
    return jnp.where(lax.axis_index("span") == tile // in_span, mine_ref[rows], other_ref[rows])


def middle_kernel(
    layer,
    arrived_ref,
    mine_ref,
    coeffs_ref,
    up_ref,
    down_ref,
    next_ref,
    sent_ref,
    band_ref,
    other_ref,
    band_in,
    mixed_ref,
    normed_ref,
    sems,
):
    own = arrived_ref.shape[3]
    tiles, steps = band_ref.shape[0], TILE // (arrived_ref.shape[2] * own)
    width = mixed_ref.shape[1]
    together = ROWS // TILE
    in_span = tiles // arrived_ref.shape[1]
    first_frame = (1 - lax.axis_index("span")) * coeffs_ref.shape[0]
    other_ref[...] = band_rows(coeffs_ref[...], first_frame, TILE // own, own)
    for tile in range(tiles):
        full = band_tile(weight_rows(tile, in_span, mine_ref, other_ref), own)
        for source in range(REACH):
            band_in[tile, source] = full[:, source * TILE : (source + 1) * TILE]
    store = copies([(band_in, band_ref)], sems)[0]
    store.start()
    for first in range(0, tiles, together):
        for place, tile in enumerate(range(first, first + together)):
            sources = [
                (
                    REACH - 1 - back,
                    arrived_ref[rows_of(arrived_ref, tile - back, steps)].reshape(TILE, width),
                )
                for back in range(min(REACH, tile + 1))
            ]
            mix(place, band_in.at[tile], sources, mixed_ref, normed_ref)
        layer_out = perceptron(mixed_ref, normed_ref, up_ref[layer], down_ref[layer])
        result = dot(layer_out, next_ref[layer + 1]).astype(jnp.bfloat16)
        result = result.reshape(together, steps, *sent_ref.shape[2:])
        for place in range(together):
            sent_ref[rows_of(sent_ref, first + place, steps)] = result[place]
    store.wait()


def row_scratch(width):
    return [pltpu.VMEM((ROWS, width), jnp.float32), pltpu.VMEM((ROWS, width), jnp.bfloat16)]


def middle_stage(layer, arrived, mine, other_coeffs, up, down, following):
    width = up.shape[1]
    snaps, spans, frames, own, _ = arrived.shape
    band = (snaps * spans * frames * own // TILE, REACH, TILE, TILE)
    return pl.pallas_call(
        functools.partial(middle_kernel, layer),
        name="middle_stage",
        out_shape=[in_vmem(arrived.shape), pltpu.HBM(band, jnp.bfloat16)],
        in_specs=vmem_specs(6),
        out_specs=vmem_specs(1) + hbm_specs(1),
        scratch_shapes=[
            pltpu.VMEM(mine.shape, jnp.float32),
            pltpu.VMEM(band, jnp.bfloat16),
            *row_scratch(width),
            pltpu.SemaphoreType.DMA((1,)),
        ],
        compiler_params=params(24),
    )(*map(held, (arrived, mine, other_coeffs, up, down, following)))


def last_kernel(
    layer, flip, arrived_ref, band_ref, up_ref, down_ref, out_ref, mixed_ref, normed_ref
):
    span = lax.axis_index("span")
    span = 1 - span if flip else span
    steps = TILE // (arrived_ref.shape[2] * arrived_ref.shape[3])
    in_span = arrived_ref.shape[0] // steps
    width = mixed_ref.shape[1]
    own = arrived_ref.shape[3]
    frames = TILE // own
    together = ROWS // TILE
    for first in range(0, in_span, together):
        for place in range(together):
            tile = span * in_span + first + place
            sources = [
                (
                    REACH - 1 - back,
                    arrived_ref[
                        rows_of(arrived_ref, jnp.maximum(tile - back, 0), steps)
                    ].reshape(TILE, width),
                )
                for back in range(REACH)
            ]
            mix(place, band_ref.at[tile], sources, mixed_ref, normed_ref)
        layer_out = perceptron(mixed_ref, normed_ref, up_ref[layer], down_ref[layer])
        out_ref[pl.ds(first * frames, together * frames)] = layer_out.reshape(
            together * frames, own, width
        )


def last_stage(layer, flip, arrived, band, up, down):
    width = up.shape[1]
    owners, _, frames, own, _ = arrived.shape
    return pl.pallas_call(
        functools.partial(last_kernel, layer, flip),
        name="last_stage",
        out_shape=in_vmem((owners * frames, own, width)),
        in_specs=vmem_specs(4),
        out_specs=pl.BlockSpec(memory_space=pltpu.VMEM),
        scratch_shapes=row_scratch(width),
        compiler_params=params(),
    )(held(arrived), held(band), held(up), held(down))


def assemble_kernel(kept_ref, received_ref, out_ref, sems):
    span = lax.axis_index("span")
    loads = copies(
        [(kept_ref, out_ref.at[:, span]), (received_ref, out_ref.at[:, 1 - span])], sems
    )
    for load in loads:
        load.start()
    for load in loads:
        load.wait()


def assemble(kept, received):
    frames, own, width = kept.shape
    return pl.pallas_call(
        assemble_kernel,
        name="assemble",
        out_shape=pltpu.HBM((frames, 2, own, width), jnp.bfloat16),
        in_specs=vmem_specs(2),
        out_specs=hbm_specs(1)[0],
        scratch_shapes=[pltpu.SemaphoreType.DMA((2,))],
        compiler_params=params(),
    )(held(kept), held(received))


def exchange(blocks):
    return lax.all_to_all(blocks, EVERY, split_axis=0, concat_axis=0, tiled=True)


def local(
    features,
    block_values,
    block_cols,
    block_counts,
    band_coeffs,
    graph_layer_weight,
    up_weight,
    down_weight,
):
    snaps, spans = lax.axis_size("snap"), lax.axis_size("span")
    span = lax.axis_index("span")
    swap = [(0, 1), (1, 0)]
    owners = snaps * spans
    frames, vertices, width = features.shape[1:]
    own = vertices // owners
    by_owner = (snaps, spans, frames, own, width)

    other_coeffs = lax.ppermute(band_coeffs[0], "span", swap)
    sent, dense, mine = first_graph(
        features,
        graph_layer_weight,
        block_values,
        block_cols,
        block_counts,
        band_coeffs,
        owners,
    )
    sent, other_coeffs = lax.optimization_barrier((sent, other_coeffs))
    for layer in range(LAYERS - 1):
        arrived = exchange(sent).reshape(by_owner)
        sent, band = middle_stage(
            layer, arrived, mine, other_coeffs, up_weight, down_weight, graph_layer_weight
        )
        arrived = exchange(sent.reshape(owners, frames, own, width))
        sent = later_graph(arrived, dense)
    arrived = exchange(sent).reshape(by_owner)
    give = last_stage(LAYERS - 1, True, arrived, band, up_weight, down_weight)
    received = lax.ppermute(give, "span", swap)
    kept = last_stage(LAYERS - 1, False, arrived, band, up_weight, down_weight)
    return assemble(kept, received).reshape(1, snaps * frames, spans * own, width)


def solution(mesh):
    in_specs = (
        P("span", "snap", None, None),
        P("span", "snap", None, None, None, None),
        P("span", "snap", None, None),
        P("span", "snap", None),
        P("span", None, None),
        P(),
        P(),
        P(),
    )
    out_specs = P("span", None, "snap", None)
    return jax.shard_map(local, mesh=mesh, in_specs=in_specs, out_specs=out_specs, check_vma=False)
```

```python
import functools

import jax
import jax.numpy as jnp
from jax import lax
from jax.experimental import pallas as pl
from jax.experimental.pallas import tpu as pltpu
from jax.sharding import PartitionSpec as P

BAND = 32
LAYERS = 2
TILE = 256
REACH = 3
ROWS = 512
GROUP = 16
OUTER = 4
MIB = 1 << 20


def dot(left, right):
    return jnp.dot(left, right, preferred_element_type=jnp.float32)


def in_vmem(shape, dtype=jnp.bfloat16):
    return pltpu.VMEM(shape, dtype)


def vmem_specs(count):
    return [pl.BlockSpec(memory_space=pltpu.VMEM)] * count


def held(array):
    return pltpu.with_memory_space_constraint(array, pltpu.VMEM)


def in_hbm(array):
    return pltpu.with_memory_space_constraint(array, pltpu.HBM)


def hbm_specs(count):
    return [pl.BlockSpec(memory_space=pltpu.HBM)] * count


def params(mib=16):
    return pltpu.CompilerParams(vmem_limit_bytes=mib * MIB)


def copies(pairs, sems):
    return [pltpu.make_async_copy(*pair, sems.at[place]) for place, pair in enumerate(pairs)]


def lay_out(frame, values_ref, cols_ref, counts_ref, dense_ref):
    block_rows, slots, size, _ = values_ref.shape[1:]
    dense_ref[frame] = jnp.zeros(dense_ref.shape[1:], dense_ref.dtype)
    for row in range(block_rows):
        for slot in reversed(range(slots)):
            column = pl.multiple_of(cols_ref[frame, row, slot] * size, size)
            block = values_ref[frame, row, slot]
            used = slot < counts_ref[frame, row]
            dense_ref[frame, pl.ds(row * size, size), pl.ds(column, size)] = jnp.where(
                used, block, jnp.zeros_like(block)
            )


def propagate(frame, dense_ref, weighted, sent_ref):
    vertices = dense_ref.shape[1]
    rows = min(vertices, 512)
    own, width = sent_ref.shape[2:]
    for first in range(0, vertices, rows):
        summed = dot(dense_ref[frame, pl.ds(first, rows)], weighted).astype(jnp.bfloat16)
        sent_ref[pl.ds(first // own, rows // own), frame] = summed.reshape(
            rows // own, own, width
        )


def band_rows(coeffs, first_frame, frames_in_tile, copies_of):
    frames = coeffs.shape[0]
    back = (REACH - 1) * frames_in_tile
    lags = lax.broadcasted_iota(jnp.int32, coeffs.shape, 1)
    here = first_frame + lax.broadcasted_iota(jnp.int32, coeffs.shape, 0)
    scaled = jnp.where(here >= lags, coeffs.astype(jnp.float32), 0.0)
    weights = scaled / jnp.sum(scaled, axis=1, keepdims=True)
    sources = REACH * frames_in_tile
    place = lax.broadcasted_iota(jnp.int32, (frames, sources), 0) % frames_in_tile
    lag = back + place - lax.broadcasted_iota(jnp.int32, (frames, sources), 1)
    chosen = jnp.zeros((frames, sources), jnp.float32)
    for each in range(BAND):
        chosen = jnp.where(lag == each, weights[:, each : each + 1], chosen)
    wide = sources * copies_of
    spread = (
        lax.broadcasted_iota(jnp.int32, (sources, wide), 1) // copies_of
        == lax.broadcasted_iota(jnp.int32, (sources, wide), 0)
    ).astype(jnp.bfloat16)
    return dot(chosen.astype(jnp.bfloat16), spread)


def first_kernel(
    features_ref,
    weight_ref,
    values_ref,
    cols_ref,
    counts_ref,
    coeffs_ref,
    sent_ref,
    spare_ref,
    dense_ref,
    band_ref,
    features_in,
    weight_in,
    values_in,
    cols_in,
    counts_in,
    coeffs_in,
    dense_in,
    sems,
):
    frames, vertices, width = features_in.shape
    loads = copies(
        [
            (coeffs_ref.at[0], coeffs_in),
            (weight_ref.at[0], weight_in),
            (features_ref.at[0], features_in),
            (cols_ref.at[0], cols_in),
            (counts_ref.at[0], counts_in),
            (values_ref.at[0], values_in),
        ],
        sems,
    )
    for load in loads:
        load.start()
    loads[0].wait()
    first_frame = lax.axis_index("span") * coeffs_in.shape[0]
    band_ref[...] = band_rows(coeffs_in[...], first_frame, TILE // GROUP, GROUP)
    for load in loads[1:3]:
        load.wait()
    weighted = dot(features_in[...].reshape(frames * vertices, width), weight_in[...])
    weighted = weighted.astype(jnp.bfloat16).reshape(frames, vertices, width)
    for load in loads[3:]:
        load.wait()
    for frame in range(frames):
        lay_out(frame, values_in, cols_in, counts_in, dense_in)
    store = pltpu.make_async_copy(dense_in, dense_ref, sems.at[len(loads)])
    store.start()
    for frame in range(frames):
        propagate(frame, dense_in, weighted[frame], sent_ref)
    store.wait()


def normed(mixed):
    mean_square = jnp.mean(mixed * mixed, axis=-1, keepdims=True)
    return (mixed * lax.rsqrt(mean_square + 1e-06)).astype(jnp.bfloat16)


def perceptron(mixed, up, down):
    active = jnp.maximum(dot(normed(mixed), up), 0.0).astype(jnp.bfloat16)
    return (mixed + dot(active, down)).astype(jnp.bfloat16)


def later_kernel(
    layer, mixed_ref, up_ref, down_ref, next_ref, dense_ref, sent_ref, spare_ref, weighted_ref
):
    _, frames, own, width = mixed_ref.shape
    vertices = dense_ref.shape[1]
    rows = min(vertices, 512)
    for frame in range(frames):
        for first in range(0, vertices, rows):
            mixed = mixed_ref[pl.ds(first // own, rows // own), frame].reshape(rows, width)
            layer_out = perceptron(mixed.astype(jnp.float32), up_ref[layer], down_ref[layer])
            weighted_ref[frame, pl.ds(first, rows)] = dot(
                layer_out, next_ref[layer + 1]
            ).astype(jnp.bfloat16)
    for frame in range(frames):
        propagate(frame, dense_ref, weighted_ref[frame], sent_ref)


def first_graph(features, weight, values, cols, counts, coeffs, owners):
    frames, vertices, width = features.shape[1:]
    own = vertices // owners
    large = 2 * (features.size + values.size + frames * vertices * vertices)
    return pl.pallas_call(
        first_kernel,
        name="first_graph",
        out_shape=[
            in_vmem((owners, frames, own, width)),
            pltpu.HBM((owners, frames, own, width), jnp.bfloat16),
            pltpu.HBM((frames, vertices, vertices), jnp.bfloat16),
            in_vmem((coeffs.shape[1], REACH * TILE), jnp.float32),
        ],
        in_specs=hbm_specs(6),
        out_specs=vmem_specs(1) + hbm_specs(2) + vmem_specs(1),
        scratch_shapes=[
            pltpu.VMEM(features.shape[1:], jnp.bfloat16),
            pltpu.VMEM(weight.shape[1:], jnp.bfloat16),
            pltpu.VMEM(values.shape[1:], jnp.bfloat16),
            pltpu.SMEM(cols.shape[1:], jnp.int32),
            pltpu.SMEM(counts.shape[1:], jnp.int32),
            pltpu.VMEM(coeffs.shape[1:], jnp.int32),
            pltpu.VMEM((frames, vertices, vertices), jnp.bfloat16),
            pltpu.SemaphoreType.DMA((7,)),
        ],
        compiler_params=params(17 + large // MIB),
    )(*map(in_hbm, (features, weight, values, cols, counts, coeffs)))


def later_graph(layer, mixed, up, down, following, dense):
    _, frames, _, width = mixed.shape
    return pl.pallas_call(
        functools.partial(later_kernel, layer),
        name="later_graph",
        out_shape=[in_vmem(mixed.shape), pltpu.HBM(mixed.shape, jnp.bfloat16)],
        in_specs=vmem_specs(5),
        out_specs=vmem_specs(1) + hbm_specs(1),
        scratch_shapes=[pltpu.VMEM((frames, dense.shape[1], width), jnp.bfloat16)],
        compiler_params=params(),
    )(*map(held, (mixed, up, down, following, dense)))


def band_tile(rows):
    frames, wide = rows.shape
    full = jnp.broadcast_to(rows[:, None, :], (frames, GROUP, wide)).reshape(
        frames * GROUP, wide
    )
    same = (
        lax.broadcasted_iota(jnp.int32, full.shape, 0) % GROUP
        == lax.broadcasted_iota(jnp.int32, full.shape, 1) % GROUP
    )
    return jnp.where(same, full, 0.0).astype(jnp.bfloat16)


def spread(weights_ref, band_ref):
    in_tile = TILE // GROUP
    for tile in range(band_ref.shape[0]):
        full = band_tile(weights_ref[pl.ds(tile * in_tile, in_tile)])
        for source in range(REACH):
            band_ref[tile, source] = full[:, source * TILE : (source + 1) * TILE]


def tile_index(ref, tile, group):
    steps = TILE // (GROUP * ref.shape[1])
    return (pl.ds(tile * steps, steps), slice(None), pl.ds(group * GROUP, GROUP))


def mix(tile, group, arrived_ref, halo_ref, band_ref):
    before = REACH - 1
    total = None
    for part in range(REACH):
        source = tile + part - before
        ref, source = (arrived_ref, source) if source >= 0 else (halo_ref, source + before)
        rows = ref[tile_index(ref, source, group)].reshape(TILE, ref.shape[3])
        term = dot(band_ref[tile, part], rows)
        total = term if total is None else total + term
    return total


def put(tile, group, rows, ref):
    index = tile_index(ref, tile, group)
    ref[index] = rows.reshape(index[0].size, ref.shape[1], GROUP, -1)


def gather_own(first_ref, second_ref, arrived_ref):
    for span, ref in enumerate((first_ref, second_ref)):

        @pl.when(lax.axis_index("span") == span)
        def own():
            arrived_ref[...] = ref[...]


def band_scratch(weights):
    return pltpu.VMEM((weights.shape[0] * GROUP // TILE, REACH, TILE, TILE), jnp.bfloat16)


def middle_kernel(
    first_ref, second_ref, halo_ref, weights_ref, sent_ref, arrived_ref, band_ref
):
    gather_own(first_ref, second_ref, arrived_ref)
    spread(weights_ref, band_ref)
    for group in range(arrived_ref.shape[2] // GROUP):
        for tile in range(band_ref.shape[0]):
            mixed = mix(tile, group, arrived_ref, halo_ref, band_ref)
            put(tile, group, mixed.astype(jnp.bfloat16), sent_ref)


def middle_stage(first, second, halo, weights):
    return pl.pallas_call(
        middle_kernel,
        name="middle_stage",
        out_shape=in_vmem(first.shape),
        in_specs=vmem_specs(4),
        out_specs=vmem_specs(1)[0],
        scratch_shapes=[pltpu.VMEM(first.shape, jnp.bfloat16), band_scratch(weights)],
        compiler_params=params(),
    )(*map(held, (first, second, halo, weights)))


def last_kernel(
    layer,
    first_ref,
    second_ref,
    halo_ref,
    weights_ref,
    up_ref,
    down_ref,
    out_ref,
    arrived_ref,
    out_in,
    down_in,
    band_ref,
    mixed_ref,
    sems,
):
    load = pltpu.make_async_copy(down_ref.at[layer], down_in, sems.at[0])
    load.start()
    gather_own(first_ref, second_ref, arrived_ref)
    spread(weights_ref, band_ref)
    groups = arrived_ref.shape[2] // GROUP
    places = [(slice(None), slice(None), pl.ds(group * GROUP, GROUP)) for group in range(groups)]
    stores = copies(
        [(out_in.at[place], out_ref.at[place]) for place in places], sems.at[pl.ds(1, groups)]
    )
    together = ROWS // TILE
    waited = False
    for group in range(groups):
        for first in range(0, band_ref.shape[0], together):
            tiles = range(first, first + together)
            for place, tile in enumerate(tiles):
                mixed_ref[pl.ds(place * TILE, TILE)] = mix(
                    tile, group, arrived_ref, halo_ref, band_ref
                )
            if not waited:
                load.wait()
                waited = True
            result = perceptron(mixed_ref[...], up_ref[layer], down_in[...])
            for place, tile in enumerate(tiles):
                put(tile, group, result[place * TILE : (place + 1) * TILE], out_in)
        stores[group].start()
    for store in stores:
        store.wait()


def last_stage(layer, first, second, halo, weights, up, down):
    groups = first.shape[2] // GROUP
    return pl.pallas_call(
        functools.partial(last_kernel, layer),
        name="last_stage",
        out_shape=pltpu.HBM(first.shape, jnp.bfloat16),
        in_specs=vmem_specs(5) + hbm_specs(1),
        out_specs=hbm_specs(1)[0],
        scratch_shapes=[
            pltpu.VMEM(first.shape, jnp.bfloat16),
            pltpu.VMEM(first.shape, jnp.bfloat16),
            pltpu.VMEM(down.shape[1:], jnp.bfloat16),
            band_scratch(weights),
            pltpu.VMEM((ROWS, up.shape[1]), jnp.float32),
            pltpu.SemaphoreType.DMA((1 + groups,)),
        ],
        compiler_params=params(20),
    )(*map(held, (first, second, halo, weights, up)), in_hbm(down))


def direct(blocks):
    return lax.all_to_all(blocks, "snap", split_axis=0, concat_axis=0, tiled=True)


def staged(blocks):
    count = blocks.shape[0]
    inner = count // OUTER
    runs = [list(range(first, first + inner)) for first in range(0, count, inner)]
    across = [list(range(first, count, inner)) for first in range(inner)]
    parted = blocks.reshape(OUTER, inner, *blocks.shape[1:])
    parted = lax.all_to_all(
        parted, "snap", split_axis=1, concat_axis=1, tiled=True, axis_index_groups=runs
    )
    parted = lax.all_to_all(
        parted, "snap", split_axis=0, concat_axis=0, tiled=True, axis_index_groups=across
    )
    return parted.reshape(blocks.shape)


def exchange_in_turn(blocks, spare, first_way, second_way):
    span = lax.axis_index("span")
    late = BAND // blocks.shape[1]
    first = lax.cond(
        span == 0, lambda blocks, spare: first_way(blocks), lambda blocks, spare: spare, blocks, spare
    )
    halo = lax.ppermute(first[-late:], "span", [(0, 1)])
    blocks, _ = lax.optimization_barrier((blocks, first))
    second = lax.cond(span == 0, lambda blocks: blocks, second_way, blocks)
    return first, second, halo


def local(
    features,
    block_values,
    block_cols,
    block_counts,
    band_coeffs,
    graph_layer_weight,
    up_weight,
    down_weight,
):
    snaps = lax.axis_size("snap")
    frames, vertices, width = features.shape[1:]
    sent, spare, dense, weights = first_graph(
        features,
        graph_layer_weight,
        block_values,
        block_cols,
        block_counts,
        band_coeffs,
        snaps,
    )
    for layer in range(LAYERS - 1):
        arrived = exchange_in_turn(sent, spare, direct, staged)
        mixed = direct(middle_stage(*arrived, weights))
        sent, spare = later_graph(layer, mixed, up_weight, down_weight, graph_layer_weight, dense)
    arrived = exchange_in_turn(sent, spare, direct, direct)
    out = last_stage(LAYERS - 1, *arrived, weights, up_weight, down_weight)
    return out.reshape(1, snaps * frames, vertices // snaps, width)


def solution(mesh):
    in_specs = (
        P("span", "snap", None, None),
        P("span", "snap", None, None, None, None),
        P("span", "snap", None, None),
        P("span", "snap", None),
        P("span", None, None),
        P(),
        P(),
        P(),
    )
    out_specs = P("span", None, "snap", None)
    return jax.shard_map(local, mesh=mesh, in_specs=in_specs, out_specs=out_specs, check_vma=False)
```

```python
import functools

import jax
import jax.numpy as jnp
from jax import lax
from jax.experimental import pallas as pl
from jax.experimental.pallas import tpu as pltpu
from jax.sharding import PartitionSpec as P

BAND = 32
LAYERS = 2
TILE = 256
REACH = 3
ROWS = 512
GROUP = 16
OUTER = 4
MIB = 1 << 20


def dot(left, right):
    return jnp.dot(left, right, preferred_element_type=jnp.float32)


def in_vmem(shape, dtype=jnp.bfloat16):
    return pltpu.VMEM(shape, dtype)


def vmem_specs(count):
    return [pl.BlockSpec(memory_space=pltpu.VMEM)] * count


def held(array):
    return pltpu.with_memory_space_constraint(array, pltpu.VMEM)


def in_hbm(array):
    return pltpu.with_memory_space_constraint(array, pltpu.HBM)


def hbm_specs(count):
    return [pl.BlockSpec(memory_space=pltpu.HBM)] * count


def params(mib=16):
    return pltpu.CompilerParams(vmem_limit_bytes=mib * MIB)


def copies(pairs, sems):
    return [pltpu.make_async_copy(*pair, sems.at[place]) for place, pair in enumerate(pairs)]


def lay_out(frame, values_ref, cols_ref, counts_ref, dense_ref):
    block_rows, slots, size, _ = values_ref.shape[1:]
    dense_ref[frame] = jnp.zeros(dense_ref.shape[1:], dense_ref.dtype)
    for row in range(block_rows):
        for slot in reversed(range(slots)):
            column = pl.multiple_of(cols_ref[frame, row, slot] * size, size)
            block = values_ref[frame, row, slot]
            used = slot < counts_ref[frame, row]
            dense_ref[frame, pl.ds(row * size, size), pl.ds(column, size)] = jnp.where(
                used, block, jnp.zeros_like(block)
            )


def propagate(frame, dense_ref, weighted, sent_ref):
    vertices = dense_ref.shape[1]
    rows = min(vertices, 512)
    own, width = sent_ref.shape[2:]
    for first in range(0, vertices, rows):
        summed = dot(dense_ref[frame, pl.ds(first, rows)], weighted).astype(jnp.bfloat16)
        sent_ref[pl.ds(first // own, rows // own), frame] = summed.reshape(
            rows // own, own, width
        )


def band_rows(coeffs, first_frame, frames_in_tile, copies_of):
    frames = coeffs.shape[0]
    back = (REACH - 1) * frames_in_tile
    lags = lax.broadcasted_iota(jnp.int32, coeffs.shape, 1)
    here = first_frame + lax.broadcasted_iota(jnp.int32, coeffs.shape, 0)
    scaled = jnp.where(here >= lags, coeffs.astype(jnp.float32), 0.0)
    weights = scaled / jnp.sum(scaled, axis=1, keepdims=True)
    sources = REACH * frames_in_tile
    place = lax.broadcasted_iota(jnp.int32, (frames, sources), 0) % frames_in_tile
    lag = back + place - lax.broadcasted_iota(jnp.int32, (frames, sources), 1)
    chosen = jnp.zeros((frames, sources), jnp.float32)
    for each in range(BAND):
        chosen = jnp.where(lag == each, weights[:, each : each + 1], chosen)
    wide = sources * copies_of
    spread = (
        lax.broadcasted_iota(jnp.int32, (sources, wide), 1) // copies_of
        == lax.broadcasted_iota(jnp.int32, (sources, wide), 0)
    ).astype(jnp.bfloat16)
    return dot(chosen.astype(jnp.bfloat16), spread)


def first_kernel(
    features_ref,
    weight_ref,
    values_ref,
    cols_ref,
    counts_ref,
    coeffs_ref,
    sent_ref,
    dense_ref,
    band_ref,
    features_in,
    weight_in,
    values_in,
    cols_in,
    counts_in,
    coeffs_in,
    dense_in,
    sems,
):
    frames, vertices, width = features_in.shape
    loads = copies(
        [
            (coeffs_ref.at[0], coeffs_in),
            (weight_ref.at[0], weight_in),
            (features_ref.at[0], features_in),
            (cols_ref.at[0], cols_in),
            (counts_ref.at[0], counts_in),
            (values_ref.at[0], values_in),
        ],
        sems,
    )
    for load in loads:
        load.start()
    loads[0].wait()
    first_frame = lax.axis_index("span") * coeffs_in.shape[0]
    band_ref[...] = band_rows(coeffs_in[...], first_frame, TILE // GROUP, GROUP)
    for load in loads[1:3]:
        load.wait()
    weighted = dot(features_in[...].reshape(frames * vertices, width), weight_in[...])
    weighted = weighted.astype(jnp.bfloat16).reshape(frames, vertices, width)
    for load in loads[3:]:
        load.wait()
    for frame in range(frames):
        lay_out(frame, values_in, cols_in, counts_in, dense_in)
    store = pltpu.make_async_copy(dense_in, dense_ref, sems.at[len(loads)])
    store.start()
    for frame in range(frames):
        propagate(frame, dense_in, weighted[frame], sent_ref)
    store.wait()


def normed(mixed):
    mean_square = jnp.mean(mixed * mixed, axis=-1, keepdims=True)
    return (mixed * lax.rsqrt(mean_square + 1e-06)).astype(jnp.bfloat16)


def perceptron(mixed, up, down):
    active = jnp.maximum(dot(normed(mixed), up), 0.0).astype(jnp.bfloat16)
    return (mixed + dot(active, down)).astype(jnp.bfloat16)


def later_kernel(
    layer, arrived_ref, up_ref, down_ref, next_ref, dense_ref, sent_ref, spare_ref, rows_ref
):
    _, frames, own, width = arrived_ref.shape
    vertices = dense_ref.shape[1]
    rows = min(vertices, 512)
    for frame in range(frames):
        rows_ref[frame] = arrived_ref[:, frame].reshape(vertices, width)

    @pl.when(lax.axis_index("span") == 0)
    def work():
        for frame in range(frames):
            for first in range(0, vertices, rows):
                place = (frame, pl.ds(first, rows))
                mixed = rows_ref[place].astype(jnp.float32)
                rows_ref[place] = perceptron(mixed, up_ref[layer], down_ref[layer])

    for frame in range(frames):
        weighted = dot(rows_ref[frame], next_ref[layer + 1]).astype(jnp.bfloat16)
        propagate(frame, dense_ref, weighted, sent_ref)


def first_graph(features, weight, values, cols, counts, coeffs, owners):
    frames, vertices, width = features.shape[1:]
    own = vertices // owners
    large = 2 * (features.size + values.size + frames * vertices * vertices)
    return pl.pallas_call(
        first_kernel,
        name="first_graph",
        out_shape=[
            in_vmem((owners, frames, own, width)),
            pltpu.HBM((frames, vertices, vertices), jnp.bfloat16),
            in_vmem((coeffs.shape[1], REACH * TILE), jnp.float32),
        ],
        in_specs=hbm_specs(6),
        out_specs=vmem_specs(1) + hbm_specs(1) + vmem_specs(1),
        scratch_shapes=[
            pltpu.VMEM(features.shape[1:], jnp.bfloat16),
            pltpu.VMEM(weight.shape[1:], jnp.bfloat16),
            pltpu.VMEM(values.shape[1:], jnp.bfloat16),
            pltpu.SMEM(cols.shape[1:], jnp.int32),
            pltpu.SMEM(counts.shape[1:], jnp.int32),
            pltpu.VMEM(coeffs.shape[1:], jnp.int32),
            pltpu.VMEM((frames, vertices, vertices), jnp.bfloat16),
            pltpu.SemaphoreType.DMA((7,)),
        ],
        compiler_params=params(17 + large // MIB),
    )(*map(in_hbm, (features, weight, values, cols, counts, coeffs)))


def later_graph(layer, mixed, up, down, following, dense):
    _, frames, _, width = mixed.shape
    return pl.pallas_call(
        functools.partial(later_kernel, layer),
        name="later_graph",
        out_shape=[in_vmem(mixed.shape), pltpu.HBM(mixed.shape, jnp.bfloat16)],
        in_specs=vmem_specs(5),
        out_specs=vmem_specs(1) + hbm_specs(1),
        scratch_shapes=[pltpu.VMEM((frames, dense.shape[1], width), jnp.bfloat16)],
        compiler_params=params(),
    )(*map(held, (mixed, up, down, following, dense)))


def band_tile(rows):
    frames, wide = rows.shape
    full = jnp.broadcast_to(rows[:, None, :], (frames, GROUP, wide)).reshape(
        frames * GROUP, wide
    )
    same = (
        lax.broadcasted_iota(jnp.int32, full.shape, 0) % GROUP
        == lax.broadcasted_iota(jnp.int32, full.shape, 1) % GROUP
    )
    return jnp.where(same, full, 0.0).astype(jnp.bfloat16)


def spread(weights_ref, band_ref):
    in_tile = TILE // GROUP
    for tile in range(band_ref.shape[0]):
        full = band_tile(weights_ref[pl.ds(tile * in_tile, in_tile)])
        for source in range(REACH):
            band_ref[tile, source] = full[:, source * TILE : (source + 1) * TILE]


def tile_index(ref, tile, group):
    steps = TILE // (GROUP * ref.shape[1])
    return (pl.ds(tile * steps, steps), slice(None), pl.ds(group * GROUP, GROUP))


def mix(tile, group, arrived_ref, halo_ref, band_ref):
    before = REACH - 1
    total = None
    for part in range(REACH):
        source = tile + part - before
        ref, source = (arrived_ref, source) if source >= 0 else (halo_ref, source + before)
        rows = ref[tile_index(ref, source, group)].reshape(TILE, ref.shape[3])
        term = dot(band_ref[tile, part], rows)
        total = term if total is None else total + term
    return total


def put(tile, group, rows, ref):
    index = tile_index(ref, tile, group)
    ref[index] = rows.reshape(index[0].size, ref.shape[1], GROUP, -1)


def own_load(first_ref, second_ref, arrived_ref, sem, act):
    for span, ref in enumerate((first_ref, second_ref)):

        @pl.when(lax.axis_index("span") == span)
        def own():
            act(pltpu.make_async_copy(ref, arrived_ref, sem))


def begin(load):
    load.start()


def finish(load):
    load.wait()


def band_scratch(weights):
    return pltpu.VMEM((weights.shape[0] * GROUP // TILE, REACH, TILE, TILE), jnp.bfloat16)


def middle_kernel(
    layer,
    halo_ref,
    weights_ref,
    first_ref,
    second_ref,
    up_ref,
    down_ref,
    sent_ref,
    arrived_ref,
    up_in,
    down_in,
    band_ref,
    mixed_ref,
    sems,
):
    second_core = lax.axis_index("span") == 1
    loads = copies([(up_ref.at[layer], up_in), (down_ref.at[layer], down_in)], sems)
    own_load(first_ref, second_ref, arrived_ref, sems.at[2], begin)

    @pl.when(second_core)
    def load_weights():
        for load in loads:
            load.start()

    spread(weights_ref, band_ref)
    own_load(first_ref, second_ref, arrived_ref, sems.at[2], finish)
    owners, frames, own, width = arrived_ref.shape
    for group in range(own // GROUP):
        for tile in range(band_ref.shape[0]):
            put(tile, group, mix(tile, group, arrived_ref, halo_ref, band_ref), mixed_ref)

    @pl.when(second_core)
    def work():
        for load in loads:
            load.wait()
        batch = ROWS // (frames * own)
        for first in range(0, owners, batch):
            rows = pl.ds(first, batch)
            result = perceptron(mixed_ref[rows].reshape(ROWS, width), up_in[...], down_in[...])
            sent_ref[rows] = result.reshape(batch, frames, own, width)

    @pl.when(jnp.logical_not(second_core))
    def leave():
        sent_ref[...] = mixed_ref[...].astype(jnp.bfloat16)


def middle_stage(layer, first, second, halo, weights, up, down):
    return pl.pallas_call(
        functools.partial(middle_kernel, layer),
        name="middle_stage",
        out_shape=in_vmem(first.shape),
        in_specs=vmem_specs(2) + hbm_specs(4),
        out_specs=vmem_specs(1)[0],
        scratch_shapes=[
            pltpu.VMEM(first.shape, jnp.bfloat16),
            pltpu.VMEM(up.shape[1:], jnp.bfloat16),
            pltpu.VMEM(down.shape[1:], jnp.bfloat16),
            band_scratch(weights),
            pltpu.VMEM(first.shape, jnp.float32),
            pltpu.SemaphoreType.DMA((3,)),
        ],
        compiler_params=params(16 + 6 * first.size // MIB),
    )(*map(held, (halo, weights)), *map(in_hbm, (first, second, up, down)))


def last_kernel(
    layer,
    second_ref,
    halo_ref,
    weights_ref,
    up_ref,
    down_ref,
    first_ref,
    out_ref,
    arrived_ref,
    out_in,
    down_in,
    band_ref,
    mixed_ref,
    sems,
):
    load = pltpu.make_async_copy(down_ref.at[layer], down_in, sems.at[0])
    load.start()
    span = lax.axis_index("span")

    @pl.when(span == 0)
    def fetch():
        own = pltpu.make_async_copy(first_ref, arrived_ref, sems.at[1])
        own.start()
        own.wait()

    @pl.when(span == 1)
    def keep():
        arrived_ref[...] = second_ref[...]

    spread(weights_ref, band_ref)
    owners, frames, own, width = arrived_ref.shape
    for group in range(own // GROUP):
        for tile in range(band_ref.shape[0]):
            put(tile, group, mix(tile, group, arrived_ref, halo_ref, band_ref), mixed_ref)
    load.wait()
    batch = ROWS // (frames * own)
    stores = []
    for place, first in enumerate(range(0, owners, batch)):
        rows = pl.ds(first, batch)
        result = perceptron(
            mixed_ref[rows].reshape(ROWS, width), up_ref[layer], down_in[...]
        )
        out_in[rows] = result.reshape(batch, frames, own, width)
        store = pltpu.make_async_copy(out_in.at[rows], out_ref.at[rows], sems.at[2 + place])
        store.start()
        stores.append(store)
    for store in stores:
        store.wait()


def last_stage(layer, first, second, halo, weights, up, down):
    owners, frames, own, _ = first.shape
    return pl.pallas_call(
        functools.partial(last_kernel, layer),
        name="last_stage",
        out_shape=pltpu.HBM(first.shape, jnp.bfloat16),
        in_specs=vmem_specs(4) + hbm_specs(2),
        out_specs=hbm_specs(1)[0],
        scratch_shapes=[
            pltpu.VMEM(first.shape, jnp.bfloat16),
            pltpu.VMEM(first.shape, jnp.bfloat16),
            pltpu.VMEM(down.shape[1:], jnp.bfloat16),
            band_scratch(weights),
            pltpu.VMEM(first.shape, jnp.float32),
            pltpu.SemaphoreType.DMA((2 + owners * frames * own // ROWS,)),
        ],
        compiler_params=params(16 + 8 * first.size // MIB),
    )(*map(held, (second, halo, weights, up)), *map(in_hbm, (down, first)))


def direct(blocks):
    return lax.all_to_all(blocks, "snap", split_axis=0, concat_axis=0, tiled=True)


def runs_of(count):
    inner = count // OUTER
    inside = [list(range(first, first + inner)) for first in range(0, count, inner)]
    across = [list(range(first, count, inner)) for first in range(inner)]
    return inside, across


def inside_runs(blocks):
    count = blocks.shape[0]
    parted = blocks.reshape(OUTER, count // OUTER, *blocks.shape[1:])
    parted = lax.all_to_all(
        parted,
        "snap",
        split_axis=1,
        concat_axis=1,
        tiled=True,
        axis_index_groups=runs_of(count)[0],
    )
    return parted.reshape(blocks.shape)


def across_runs(blocks):
    count = blocks.shape[0]
    parted = blocks.reshape(OUTER, count // OUTER, *blocks.shape[1:])
    parted = lax.all_to_all(
        parted,
        "snap",
        split_axis=0,
        concat_axis=0,
        tiled=True,
        axis_index_groups=runs_of(count)[1],
    )
    return parted.reshape(blocks.shape)


def exchange_in_turn(blocks, second_begins, second_ends):
    span = lax.axis_index("span")
    late = BAND // blocks.shape[1]
    first = lax.cond(span == 0, direct, second_begins, blocks)
    halo = lax.ppermute(first[-late:], "span", [(0, 1)])
    blocks, begun = lax.optimization_barrier((blocks, first))
    second = lax.cond(
        span == 0,
        lambda blocks, begun: blocks,
        lambda blocks, begun: second_ends(blocks, begun),
        blocks,
        begun,
    )
    return first, second, halo


def local(
    features,
    block_values,
    block_cols,
    block_counts,
    band_coeffs,
    graph_layer_weight,
    up_weight,
    down_weight,
):
    snaps = lax.axis_size("snap")
    frames, vertices, width = features.shape[1:]
    sent, dense, weights = first_graph(
        features,
        graph_layer_weight,
        block_values,
        block_cols,
        block_counts,
        band_coeffs,
        snaps,
    )
    for layer in range(LAYERS - 1):
        arrived = exchange_in_turn(sent, inside_runs, lambda blocks, begun: across_runs(begun))
        rows = direct(middle_stage(layer, *arrived, weights, up_weight, down_weight))
        sent, spare = later_graph(layer, rows, up_weight, down_weight, graph_layer_weight, dense)
    arrived = exchange_in_turn(
        sent, lambda blocks: spare, lambda blocks, begun: direct(blocks)
    )
    out = last_stage(LAYERS - 1, *arrived, weights, up_weight, down_weight)
    return out.reshape(1, snaps * frames, vertices // snaps, width)


def solution(mesh):
    in_specs = (
        P("span", "snap", None, None),
        P("span", "snap", None, None, None, None),
        P("span", "snap", None, None),
        P("span", "snap", None),
        P("span", None, None),
        P(),
        P(),
        P(),
    )
    out_specs = P("span", None, "snap", None)
    return jax.shard_map(local, mesh=mesh, in_specs=in_specs, out_specs=out_specs, check_vma=False)
```

```python
import functools

import jax
import jax.numpy as jnp
from jax import lax
from jax.experimental import pallas as pl
from jax.experimental.pallas import tpu as pltpu
from jax.sharding import PartitionSpec as P

BAND = 32
LAYERS = 2
TILE = 256
REACH = 3
ROWS = 512
GROUP = 16
OUTER = 4
MIB = 1 << 20


def dot(left, right):
    return jnp.dot(left, right, preferred_element_type=jnp.float32)


def in_vmem(shape, dtype=jnp.bfloat16):
    return pltpu.VMEM(shape, dtype)


def vmem_specs(count):
    return [pl.BlockSpec(memory_space=pltpu.VMEM)] * count


def held(array):
    return pltpu.with_memory_space_constraint(array, pltpu.VMEM)


def in_hbm(array):
    return pltpu.with_memory_space_constraint(array, pltpu.HBM)


def hbm_specs(count):
    return [pl.BlockSpec(memory_space=pltpu.HBM)] * count


def params(mib=16):
    return pltpu.CompilerParams(vmem_limit_bytes=mib * MIB)


def copies(pairs, sems):
    return [pltpu.make_async_copy(*pair, sems.at[place]) for place, pair in enumerate(pairs)]


def lay_out(frame, values_ref, cols_ref, counts_ref, dense_ref):
    block_rows, slots, size, _ = values_ref.shape[1:]
    dense_ref[frame] = jnp.zeros(dense_ref.shape[1:], dense_ref.dtype)
    for row in range(block_rows):
        for slot in reversed(range(slots)):
            column = pl.multiple_of(cols_ref[frame, row, slot] * size, size)
            block = values_ref[frame, row, slot]
            used = slot < counts_ref[frame, row]
            dense_ref[frame, pl.ds(row * size, size), pl.ds(column, size)] = jnp.where(
                used, block, jnp.zeros_like(block)
            )


def propagate(frame, dense_ref, weighted, sent_ref):
    vertices = dense_ref.shape[1]
    rows = min(vertices, 512)
    own, width = sent_ref.shape[2:]
    for first in range(0, vertices, rows):
        summed = dot(dense_ref[frame, pl.ds(first, rows)], weighted).astype(jnp.bfloat16)
        sent_ref[pl.ds(first // own, rows // own), frame] = summed.reshape(
            rows // own, own, width
        )


def band_rows(coeffs, first_frame, frames_in_tile, copies_of):
    frames = coeffs.shape[0]
    back = (REACH - 1) * frames_in_tile
    lags = lax.broadcasted_iota(jnp.int32, coeffs.shape, 1)
    here = first_frame + lax.broadcasted_iota(jnp.int32, coeffs.shape, 0)
    scaled = jnp.where(here >= lags, coeffs.astype(jnp.float32), 0.0)
    weights = scaled / jnp.sum(scaled, axis=1, keepdims=True)
    sources = REACH * frames_in_tile
    place = lax.broadcasted_iota(jnp.int32, (frames, sources), 0) % frames_in_tile
    lag = back + place - lax.broadcasted_iota(jnp.int32, (frames, sources), 1)
    chosen = jnp.zeros((frames, sources), jnp.float32)
    for each in range(BAND):
        chosen = jnp.where(lag == each, weights[:, each : each + 1], chosen)
    wide = sources * copies_of
    spread = (
        lax.broadcasted_iota(jnp.int32, (sources, wide), 1) // copies_of
        == lax.broadcasted_iota(jnp.int32, (sources, wide), 0)
    ).astype(jnp.bfloat16)
    return dot(chosen.astype(jnp.bfloat16), spread)


def first_kernel(
    features_ref,
    weight_ref,
    values_ref,
    cols_ref,
    counts_ref,
    coeffs_ref,
    sent_ref,
    dense_ref,
    band_ref,
    features_in,
    weight_in,
    values_in,
    cols_in,
    counts_in,
    coeffs_in,
    dense_in,
    sems,
):
    frames, vertices, width = features_in.shape
    loads = copies(
        [
            (coeffs_ref.at[0], coeffs_in),
            (weight_ref.at[0], weight_in),
            (features_ref.at[0, 0], features_in.at[0]),
            (cols_ref.at[0], cols_in),
            (counts_ref.at[0], counts_in),
            (values_ref.at[0], values_in),
            *((features_ref.at[0, frame], features_in.at[frame]) for frame in range(1, frames)),
        ],
        sems,
    )
    for load in loads:
        load.start()
    loads[0].wait()
    first_frame = lax.axis_index("span") * coeffs_in.shape[0]
    band_ref[...] = band_rows(coeffs_in[...], first_frame, TILE // GROUP, GROUP)
    for load in loads[1:3]:
        load.wait()
    weighted = [dot(features_in[0], weight_in[...]).astype(jnp.bfloat16)]
    for load in loads[3:]:
        load.wait()
    for frame in range(frames):
        lay_out(frame, values_in, cols_in, counts_in, dense_in)
    for frame in range(1, frames):
        weighted.append(dot(features_in[frame], weight_in[...]).astype(jnp.bfloat16))
    store = pltpu.make_async_copy(dense_in, dense_ref, sems.at[len(loads)])
    store.start()
    for frame in range(frames):
        propagate(frame, dense_in, weighted[frame], sent_ref)
    store.wait()


def normed(mixed):
    mean_square = jnp.mean(mixed * mixed, axis=-1, keepdims=True)
    return (mixed * lax.rsqrt(mean_square + 1e-06)).astype(jnp.bfloat16)


def perceptron(mixed, up, down):
    active = jnp.maximum(dot(normed(mixed), up), 0.0).astype(jnp.bfloat16)
    return (mixed + dot(active, down)).astype(jnp.bfloat16)


def later_kernel(
    layer, arrived_ref, up_ref, down_ref, next_ref, dense_ref, sent_ref, spare_ref, rows_ref
):
    _, frames, own, width = arrived_ref.shape
    vertices = dense_ref.shape[1]
    batch = ROWS // (frames * own)
    span = lax.axis_index("span")

    @pl.when(span == 0)
    def work():
        for first in range(0, arrived_ref.shape[0], batch):
            mixed = arrived_ref[pl.ds(first, batch)].reshape(ROWS, width)
            done = perceptron(mixed.astype(jnp.float32), up_ref[layer], down_ref[layer])
            done = done.reshape(batch, frames, own, width)
            for frame in range(frames):
                rows_ref[frame, pl.ds(first * own, batch * own)] = done[:, frame].reshape(
                    batch * own, width
                )

    @pl.when(span == 1)
    def gather():
        for frame in range(frames):
            rows_ref[frame] = arrived_ref[:, frame].reshape(vertices, width)

    for frame in range(frames):
        weighted = dot(rows_ref[frame], next_ref[layer + 1]).astype(jnp.bfloat16)
        propagate(frame, dense_ref, weighted, sent_ref)


def first_graph(features, weight, values, cols, counts, coeffs, owners):
    frames, vertices, width = features.shape[1:]
    own = vertices // owners
    large = 2 * (features.size + values.size + frames * vertices * vertices)
    return pl.pallas_call(
        first_kernel,
        name="first_graph",
        out_shape=[
            in_vmem((owners, frames, own, width)),
            pltpu.HBM((frames, vertices, vertices), jnp.bfloat16),
            in_vmem((coeffs.shape[1], REACH * TILE), jnp.float32),
        ],
        in_specs=hbm_specs(6),
        out_specs=vmem_specs(1) + hbm_specs(1) + vmem_specs(1),
        scratch_shapes=[
            pltpu.VMEM(features.shape[1:], jnp.bfloat16),
            pltpu.VMEM(weight.shape[1:], jnp.bfloat16),
            pltpu.VMEM(values.shape[1:], jnp.bfloat16),
            pltpu.SMEM(cols.shape[1:], jnp.int32),
            pltpu.SMEM(counts.shape[1:], jnp.int32),
            pltpu.VMEM(coeffs.shape[1:], jnp.int32),
            pltpu.VMEM((frames, vertices, vertices), jnp.bfloat16),
            pltpu.SemaphoreType.DMA((6 + frames,)),
        ],
        compiler_params=params(17 + large // MIB),
    )(*map(in_hbm, (features, weight, values, cols, counts, coeffs)))


def later_graph(layer, mixed, up, down, following, dense):
    _, frames, _, width = mixed.shape
    return pl.pallas_call(
        functools.partial(later_kernel, layer),
        name="later_graph",
        out_shape=[in_vmem(mixed.shape), pltpu.HBM(mixed.shape, jnp.bfloat16)],
        in_specs=vmem_specs(5),
        out_specs=vmem_specs(1) + hbm_specs(1),
        scratch_shapes=[pltpu.VMEM((frames, dense.shape[1], width), jnp.bfloat16)],
        compiler_params=params(),
    )(*map(held, (mixed, up, down, following, dense)))


def band_tile(rows):
    frames, wide = rows.shape
    full = jnp.broadcast_to(rows[:, None, :], (frames, GROUP, wide)).reshape(
        frames * GROUP, wide
    )
    same = (
        lax.broadcasted_iota(jnp.int32, full.shape, 0) % GROUP
        == lax.broadcasted_iota(jnp.int32, full.shape, 1) % GROUP
    )
    return jnp.where(same, full, 0.0).astype(jnp.bfloat16)


def spread(weights_ref, band_ref):
    in_tile = TILE // GROUP
    for tile in range(band_ref.shape[0]):
        full = band_tile(weights_ref[pl.ds(tile * in_tile, in_tile)])
        for source in range(REACH):
            band_ref[tile, source] = full[:, source * TILE : (source + 1) * TILE]


def tile_index(ref, tile, group):
    steps = TILE // (GROUP * ref.shape[1])
    return (pl.ds(tile * steps, steps), slice(None), pl.ds(group * GROUP, GROUP))


def mix(tile, group, arrived_ref, halo_ref, band_ref):
    before = REACH - 1
    total = None
    for part in range(REACH):
        source = tile + part - before
        ref, source = (arrived_ref, source) if source >= 0 else (halo_ref, source + before)
        rows = ref[tile_index(ref, source, group)].reshape(TILE, ref.shape[3])
        term = dot(band_ref[tile, part], rows)
        total = term if total is None else total + term
    return total


def put(tile, group, rows, ref):
    index = tile_index(ref, tile, group)
    ref[index] = rows.reshape(index[0].size, ref.shape[1], GROUP, -1)


def keep_first(first_ref, arrived_ref):
    @pl.when(lax.axis_index("span") == 0)
    def keep():
        arrived_ref[...] = first_ref[...]


def band_scratch(weights):
    return pltpu.VMEM((weights.shape[0] * GROUP // TILE, REACH, TILE, TILE), jnp.bfloat16)


def middle_kernel(
    layer,
    first_ref,
    halo_ref,
    weights_ref,
    second_ref,
    up_ref,
    down_ref,
    sent_ref,
    arrived_ref,
    up_in,
    down_in,
    band_ref,
    mixed_ref,
    sems,
):
    second_core = lax.axis_index("span") == 1
    loads = copies(
        [
            (second_ref, arrived_ref),
            (up_ref.at[layer], up_in),
            (down_ref.at[layer], down_in),
        ],
        sems,
    )

    @pl.when(second_core)
    def load_own():
        for load in loads:
            load.start()

    spread(weights_ref, band_ref)
    keep_first(first_ref, arrived_ref)

    @pl.when(second_core)
    def wait_own():
        loads[0].wait()

    owners, frames, own, width = arrived_ref.shape
    for group in range(own // GROUP):
        for tile in range(band_ref.shape[0]):
            put(tile, group, mix(tile, group, arrived_ref, halo_ref, band_ref), mixed_ref)

    @pl.when(second_core)
    def work():
        for load in loads[1:]:
            load.wait()
        batch = ROWS // (frames * own)
        for first in range(0, owners, batch):
            rows = pl.ds(first, batch)
            result = perceptron(mixed_ref[rows].reshape(ROWS, width), up_in[...], down_in[...])
            sent_ref[rows] = result.reshape(batch, frames, own, width)

    @pl.when(jnp.logical_not(second_core))
    def leave():
        sent_ref[...] = mixed_ref[...].astype(jnp.bfloat16)


def middle_stage(layer, first, second, halo, weights, up, down):
    return pl.pallas_call(
        functools.partial(middle_kernel, layer),
        name="middle_stage",
        out_shape=in_vmem(first.shape),
        in_specs=vmem_specs(3) + hbm_specs(3),
        out_specs=vmem_specs(1)[0],
        scratch_shapes=[
            pltpu.VMEM(first.shape, jnp.bfloat16),
            pltpu.VMEM(up.shape[1:], jnp.bfloat16),
            pltpu.VMEM(down.shape[1:], jnp.bfloat16),
            band_scratch(weights),
            pltpu.VMEM(first.shape, jnp.float32),
            pltpu.SemaphoreType.DMA((3,)),
        ],
        compiler_params=params(16 + 6 * first.size // MIB),
    )(*map(held, (first, halo, weights)), *map(in_hbm, (second, up, down)))


def last_kernel(
    layer,
    second_ref,
    halo_ref,
    weights_ref,
    up_ref,
    down_ref,
    first_ref,
    out_ref,
    arrived_ref,
    out_in,
    down_in,
    band_ref,
    mixed_ref,
    sems,
):
    load = pltpu.make_async_copy(down_ref.at[layer], down_in, sems.at[0])
    load.start()
    span = lax.axis_index("span")

    @pl.when(span == 0)
    def fetch():
        own = pltpu.make_async_copy(first_ref, arrived_ref, sems.at[1])
        own.start()
        own.wait()

    @pl.when(span == 1)
    def keep():
        arrived_ref[...] = second_ref[...]

    spread(weights_ref, band_ref)
    owners, frames, own, width = arrived_ref.shape
    for group in range(own // GROUP):
        for tile in range(band_ref.shape[0]):
            put(tile, group, mix(tile, group, arrived_ref, halo_ref, band_ref), mixed_ref)
    load.wait()
    batch = ROWS // (frames * own)
    stores = []
    for place, first in enumerate(range(0, owners, batch)):
        rows = pl.ds(first, batch)
        result = perceptron(
            mixed_ref[rows].reshape(ROWS, width), up_ref[layer], down_in[...]
        )
        out_in[rows] = result.reshape(batch, frames, own, width)
        store = pltpu.make_async_copy(out_in.at[rows], out_ref.at[rows], sems.at[2 + place])
        store.start()
        stores.append(store)
    for store in stores:
        store.wait()


def last_stage(layer, first, second, halo, weights, up, down):
    owners, frames, own, _ = first.shape
    return pl.pallas_call(
        functools.partial(last_kernel, layer),
        name="last_stage",
        out_shape=pltpu.HBM(first.shape, jnp.bfloat16),
        in_specs=vmem_specs(4) + hbm_specs(2),
        out_specs=hbm_specs(1)[0],
        scratch_shapes=[
            pltpu.VMEM(first.shape, jnp.bfloat16),
            pltpu.VMEM(first.shape, jnp.bfloat16),
            pltpu.VMEM(down.shape[1:], jnp.bfloat16),
            band_scratch(weights),
            pltpu.VMEM(first.shape, jnp.float32),
            pltpu.SemaphoreType.DMA((2 + owners * frames * own // ROWS,)),
        ],
        compiler_params=params(16 + 8 * first.size // MIB),
    )(*map(held, (second, halo, weights, up)), *map(in_hbm, (down, first)))


def direct(blocks):
    return lax.all_to_all(blocks, "snap", split_axis=0, concat_axis=0, tiled=True)


def runs_of(count):
    inner = count // OUTER
    inside = [list(range(first, first + inner)) for first in range(0, count, inner)]
    across = [list(range(first, count, inner)) for first in range(inner)]
    return inside, across


def inside_runs(blocks):
    count = blocks.shape[0]
    parted = blocks.reshape(OUTER, count // OUTER, *blocks.shape[1:])
    parted = lax.all_to_all(
        parted,
        "snap",
        split_axis=1,
        concat_axis=1,
        tiled=True,
        axis_index_groups=runs_of(count)[0],
    )
    return parted.reshape(blocks.shape)


def across_runs(blocks):
    count = blocks.shape[0]
    parted = blocks.reshape(OUTER, count // OUTER, *blocks.shape[1:])
    parted = lax.all_to_all(
        parted,
        "snap",
        split_axis=0,
        concat_axis=0,
        tiled=True,
        axis_index_groups=runs_of(count)[1],
    )
    return parted.reshape(blocks.shape)


def exchange_in_turn(blocks, second_begins, second_ends):
    span = lax.axis_index("span")
    late = BAND // blocks.shape[1]
    first = lax.cond(span == 0, direct, second_begins, blocks)
    halo = lax.ppermute(first[-late:], "span", [(0, 1)])
    blocks, begun = lax.optimization_barrier((blocks, first))
    second = lax.cond(
        span == 0,
        lambda blocks, begun: blocks,
        lambda blocks, begun: second_ends(blocks, begun),
        blocks,
        begun,
    )
    return first, second, halo


def local(
    features,
    block_values,
    block_cols,
    block_counts,
    band_coeffs,
    graph_layer_weight,
    up_weight,
    down_weight,
):
    snaps = lax.axis_size("snap")
    frames, vertices, width = features.shape[1:]
    sent, dense, weights = first_graph(
        features,
        graph_layer_weight,
        block_values,
        block_cols,
        block_counts,
        band_coeffs,
        snaps,
    )
    for layer in range(LAYERS - 1):
        arrived = exchange_in_turn(sent, inside_runs, lambda blocks, begun: across_runs(begun))
        rows = direct(middle_stage(layer, *arrived, weights, up_weight, down_weight))
        sent, spare = later_graph(layer, rows, up_weight, down_weight, graph_layer_weight, dense)
    arrived = exchange_in_turn(
        sent, lambda blocks: spare, lambda blocks, begun: direct(blocks)
    )
    out = last_stage(LAYERS - 1, *arrived, weights, up_weight, down_weight)
    return out.reshape(1, snaps * frames, vertices // snaps, width)


def solution(mesh):
    in_specs = (
        P("span", "snap", None, None),
        P("span", "snap", None, None, None, None),
        P("span", "snap", None, None),
        P("span", "snap", None),
        P("span", None, None),
        P(),
        P(),
        P(),
    )
    out_specs = P("span", None, "snap", None)
    return jax.shard_map(local, mesh=mesh, in_specs=in_specs, out_specs=out_specs, check_vma=False)
```

```python
import functools

import jax
import jax.numpy as jnp
from jax import lax
from jax.experimental import pallas as pl
from jax.experimental.pallas import tpu as pltpu
from jax.sharding import PartitionSpec as P

BAND = 32
LAYERS = 2
TILE = 256
REACH = 3
ROWS = 512
GROUP = 16
OUTER = 4
MIB = 1 << 20


def dot(left, right):
    return jnp.dot(left, right, preferred_element_type=jnp.float32)


def in_vmem(shape, dtype=jnp.bfloat16):
    return pltpu.VMEM(shape, dtype)


def vmem_specs(count):
    return [pl.BlockSpec(memory_space=pltpu.VMEM)] * count


def held(array):
    return pltpu.with_memory_space_constraint(array, pltpu.VMEM)


def in_hbm(array):
    return pltpu.with_memory_space_constraint(array, pltpu.HBM)


def hbm_specs(count):
    return [pl.BlockSpec(memory_space=pltpu.HBM)] * count


def params(mib=16):
    return pltpu.CompilerParams(vmem_limit_bytes=mib * MIB)


def copies(pairs, sems):
    return [pltpu.make_async_copy(*pair, sems.at[place]) for place, pair in enumerate(pairs)]


def lay_out(frame, values_ref, cols_ref, counts_ref, dense_ref):
    block_rows, slots, size, _ = values_ref.shape[1:]
    dense_ref[frame] = jnp.zeros(dense_ref.shape[1:], dense_ref.dtype)
    for row in range(block_rows):
        for slot in reversed(range(slots)):
            column = pl.multiple_of(cols_ref[frame, row, slot] * size, size)
            block = values_ref[frame, row, slot]
            used = slot < counts_ref[frame, row]
            dense_ref[frame, pl.ds(row * size, size), pl.ds(column, size)] = jnp.where(
                used, block, jnp.zeros_like(block)
            )


def propagate(frame, dense_ref, weighted, sent_ref):
    vertices = dense_ref.shape[1]
    rows = min(vertices, 512)
    own, width = sent_ref.shape[2:]
    for first in range(0, vertices, rows):
        summed = dot(dense_ref[frame, pl.ds(first, rows)], weighted).astype(jnp.bfloat16)
        sent_ref[pl.ds(first // own, rows // own), frame] = summed.reshape(
            rows // own, own, width
        )


def band_rows(coeffs, first_frame, frames_in_tile, copies_of):
    frames = coeffs.shape[0]
    back = (REACH - 1) * frames_in_tile
    lags = lax.broadcasted_iota(jnp.int32, coeffs.shape, 1)
    here = first_frame + lax.broadcasted_iota(jnp.int32, coeffs.shape, 0)
    scaled = jnp.where(here >= lags, coeffs.astype(jnp.float32), 0.0)
    weights = scaled / jnp.sum(scaled, axis=1, keepdims=True)
    sources = REACH * frames_in_tile
    place = lax.broadcasted_iota(jnp.int32, (frames, sources), 0) % frames_in_tile
    lag = back + place - lax.broadcasted_iota(jnp.int32, (frames, sources), 1)
    chosen = jnp.zeros((frames, sources), jnp.float32)
    for each in range(BAND):
        chosen = jnp.where(lag == each, weights[:, each : each + 1], chosen)
    wide = sources * copies_of
    spread = (
        lax.broadcasted_iota(jnp.int32, (sources, wide), 1) // copies_of
        == lax.broadcasted_iota(jnp.int32, (sources, wide), 0)
    ).astype(jnp.bfloat16)
    return dot(chosen.astype(jnp.bfloat16), spread)


def first_kernel(
    features_ref,
    weight_ref,
    values_ref,
    cols_ref,
    counts_ref,
    coeffs_ref,
    sent_ref,
    dense_ref,
    band_ref,
    features_in,
    weight_in,
    values_in,
    cols_in,
    counts_in,
    coeffs_in,
    dense_in,
    sems,
):
    frames, vertices, width = features_in.shape
    loads = copies(
        [
            (coeffs_ref.at[0], coeffs_in),
            (weight_ref.at[0], weight_in),
            (features_ref.at[0, 0], features_in.at[0]),
            (cols_ref.at[0], cols_in),
            (counts_ref.at[0], counts_in),
            (values_ref.at[0], values_in),
            *((features_ref.at[0, frame], features_in.at[frame]) for frame in range(1, frames)),
        ],
        sems,
    )
    for load in loads:
        load.start()
    loads[0].wait()
    first_frame = lax.axis_index("span") * coeffs_in.shape[0]
    band_ref[...] = band_rows(coeffs_in[...], first_frame, TILE // GROUP, GROUP)
    for load in loads[1:3]:
        load.wait()
    weighted = [dot(features_in[0], weight_in[...]).astype(jnp.bfloat16)]
    for load in loads[3:]:
        load.wait()
    for frame in range(frames):
        lay_out(frame, values_in, cols_in, counts_in, dense_in)
    for frame in range(1, frames):
        weighted.append(dot(features_in[frame], weight_in[...]).astype(jnp.bfloat16))
    store = pltpu.make_async_copy(dense_in, dense_ref, sems.at[len(loads)])
    store.start()
    for frame in range(frames):
        propagate(frame, dense_in, weighted[frame], sent_ref)
    store.wait()


def normed(mixed):
    mean_square = jnp.mean(mixed * mixed, axis=-1, keepdims=True)
    return (mixed * lax.rsqrt(mean_square + 1e-06)).astype(jnp.bfloat16)


def perceptron(mixed, up, down):
    active = jnp.maximum(dot(normed(mixed), up), 0.0).astype(jnp.bfloat16)
    return (mixed + dot(active, down)).astype(jnp.bfloat16)


def later_kernel(
    layer, arrived_ref, up_ref, down_ref, next_ref, dense_ref, sent_ref, spare_ref, rows_ref
):
    _, frames, own, width = arrived_ref.shape
    vertices = dense_ref.shape[1]
    batch = ROWS // (frames * own)
    span = lax.axis_index("span")

    @pl.when(span == 0)
    def work():
        for first in range(0, arrived_ref.shape[0], batch):
            mixed = arrived_ref[pl.ds(first, batch)].reshape(ROWS, width)
            done = perceptron(mixed.astype(jnp.float32), up_ref[layer], down_ref[layer])
            done = done.reshape(batch, frames, own, width)
            for frame in range(frames):
                rows_ref[frame, pl.ds(first * own, batch * own)] = done[:, frame].reshape(
                    batch * own, width
                )

    @pl.when(span == 1)
    def gather():
        for frame in range(frames):
            rows_ref[frame] = arrived_ref[:, frame].reshape(vertices, width)

    weighted = dot(rows_ref[...].reshape(frames * vertices, width), next_ref[layer + 1])
    weighted = weighted.astype(jnp.bfloat16).reshape(frames, vertices, width)
    for frame in range(frames):
        propagate(frame, dense_ref, weighted[frame], sent_ref)


def first_graph(features, weight, values, cols, counts, coeffs, owners):
    frames, vertices, width = features.shape[1:]
    own = vertices // owners
    large = 2 * (features.size + values.size + frames * vertices * vertices)
    return pl.pallas_call(
        first_kernel,
        name="first_graph",
        out_shape=[
            in_vmem((owners, frames, own, width)),
            pltpu.HBM((frames, vertices, vertices), jnp.bfloat16),
            in_vmem((coeffs.shape[1], REACH * TILE), jnp.float32),
        ],
        in_specs=hbm_specs(6),
        out_specs=vmem_specs(1) + hbm_specs(1) + vmem_specs(1),
        scratch_shapes=[
            pltpu.VMEM(features.shape[1:], jnp.bfloat16),
            pltpu.VMEM(weight.shape[1:], jnp.bfloat16),
            pltpu.VMEM(values.shape[1:], jnp.bfloat16),
            pltpu.SMEM(cols.shape[1:], jnp.int32),
            pltpu.SMEM(counts.shape[1:], jnp.int32),
            pltpu.VMEM(coeffs.shape[1:], jnp.int32),
            pltpu.VMEM((frames, vertices, vertices), jnp.bfloat16),
            pltpu.SemaphoreType.DMA((6 + frames,)),
        ],
        compiler_params=params(17 + large // MIB),
    )(*map(in_hbm, (features, weight, values, cols, counts, coeffs)))


def later_graph(layer, mixed, up, down, following, dense):
    _, frames, _, width = mixed.shape
    return pl.pallas_call(
        functools.partial(later_kernel, layer),
        name="later_graph",
        out_shape=[in_vmem(mixed.shape), pltpu.HBM(mixed.shape, jnp.bfloat16)],
        in_specs=vmem_specs(5),
        out_specs=vmem_specs(1) + hbm_specs(1),
        scratch_shapes=[pltpu.VMEM((frames, dense.shape[1], width), jnp.bfloat16)],
        compiler_params=params(),
    )(*map(held, (mixed, up, down, following, dense)))


def band_tile(rows):
    frames, wide = rows.shape
    full = jnp.broadcast_to(rows[:, None, :], (frames, GROUP, wide)).reshape(
        frames * GROUP, wide
    )
    same = (
        lax.broadcasted_iota(jnp.int32, full.shape, 0) % GROUP
        == lax.broadcasted_iota(jnp.int32, full.shape, 1) % GROUP
    )
    return jnp.where(same, full, 0.0).astype(jnp.bfloat16)


def spread(weights_ref, band_ref):
    in_tile = TILE // GROUP
    for tile in range(band_ref.shape[0]):
        full = band_tile(weights_ref[pl.ds(tile * in_tile, in_tile)])
        for source in range(REACH):
            band_ref[tile, source] = full[:, source * TILE : (source + 1) * TILE]


def tile_index(ref, tile, group):
    steps = TILE // (GROUP * ref.shape[1])
    return (pl.ds(tile * steps, steps), slice(None), pl.ds(group * GROUP, GROUP))


def mix(tile, group, arrived_ref, halo_ref, band_ref):
    before = REACH - 1
    total = None
    for part in range(REACH):
        source = tile + part - before
        ref, source = (arrived_ref, source) if source >= 0 else (halo_ref, source + before)
        rows = ref[tile_index(ref, source, group)].reshape(TILE, ref.shape[3])
        term = dot(band_ref[tile, part], rows)
        total = term if total is None else total + term
    return total


def put(tile, group, rows, ref):
    index = tile_index(ref, tile, group)
    ref[index] = rows.reshape(index[0].size, ref.shape[1], GROUP, -1)


def keep_first(first_ref, arrived_ref):
    @pl.when(lax.axis_index("span") == 0)
    def keep():
        arrived_ref[...] = first_ref[...]


def band_scratch(weights):
    return pltpu.VMEM((weights.shape[0] * GROUP // TILE, REACH, TILE, TILE), jnp.bfloat16)


def middle_kernel(
    layer,
    first_ref,
    halo_ref,
    weights_ref,
    second_ref,
    up_ref,
    down_ref,
    sent_ref,
    arrived_ref,
    up_in,
    down_in,
    band_ref,
    mixed_ref,
    sems,
):
    second_core = lax.axis_index("span") == 1
    loads = copies(
        [
            (second_ref, arrived_ref),
            (up_ref.at[layer], up_in),
            (down_ref.at[layer], down_in),
        ],
        sems,
    )

    @pl.when(second_core)
    def load_own():
        for load in loads:
            load.start()

    spread(weights_ref, band_ref)
    keep_first(first_ref, arrived_ref)

    @pl.when(second_core)
    def wait_own():
        loads[0].wait()

    owners, frames, own, width = arrived_ref.shape
    for group in range(own // GROUP):
        for tile in range(band_ref.shape[0]):
            put(tile, group, mix(tile, group, arrived_ref, halo_ref, band_ref), mixed_ref)

    @pl.when(second_core)
    def work():
        for load in loads[1:]:
            load.wait()
        batch = ROWS // (frames * own)
        for first in range(0, owners, batch):
            rows = pl.ds(first, batch)
            result = perceptron(mixed_ref[rows].reshape(ROWS, width), up_in[...], down_in[...])
            sent_ref[rows] = result.reshape(batch, frames, own, width)

    @pl.when(jnp.logical_not(second_core))
    def leave():
        sent_ref[...] = mixed_ref[...].astype(jnp.bfloat16)


def middle_stage(layer, first, second, halo, weights, up, down):
    return pl.pallas_call(
        functools.partial(middle_kernel, layer),
        name="middle_stage",
        out_shape=in_vmem(first.shape),
        in_specs=vmem_specs(3) + hbm_specs(3),
        out_specs=vmem_specs(1)[0],
        scratch_shapes=[
            pltpu.VMEM(first.shape, jnp.bfloat16),
            pltpu.VMEM(up.shape[1:], jnp.bfloat16),
            pltpu.VMEM(down.shape[1:], jnp.bfloat16),
            band_scratch(weights),
            pltpu.VMEM(first.shape, jnp.float32),
            pltpu.SemaphoreType.DMA((3,)),
        ],
        compiler_params=params(16 + 6 * first.size // MIB),
    )(*map(held, (first, halo, weights)), *map(in_hbm, (second, up, down)))


def last_kernel(
    layer,
    second_ref,
    halo_ref,
    weights_ref,
    up_ref,
    down_ref,
    first_ref,
    out_ref,
    arrived_ref,
    out_in,
    down_in,
    band_ref,
    mixed_ref,
    sems,
):
    load = pltpu.make_async_copy(down_ref.at[layer], down_in, sems.at[0])
    load.start()
    span = lax.axis_index("span")

    @pl.when(span == 0)
    def fetch():
        own = pltpu.make_async_copy(first_ref, arrived_ref, sems.at[1])
        own.start()
        own.wait()

    @pl.when(span == 1)
    def keep():
        arrived_ref[...] = second_ref[...]

    spread(weights_ref, band_ref)
    owners, frames, own, width = arrived_ref.shape
    for group in range(own // GROUP):
        for tile in range(band_ref.shape[0]):
            put(tile, group, mix(tile, group, arrived_ref, halo_ref, band_ref), mixed_ref)
    load.wait()
    batch = ROWS // (frames * own)
    parts = [(first, batch) for first in range(0, owners - batch, batch)]
    parts += [(owners - batch, batch // 2), (owners - batch // 2, batch // 2)]
    stores = []
    for place, (first, count) in enumerate(parts):
        rows = pl.ds(first, count)
        mixed = mixed_ref[rows].reshape(count * frames * own, width)
        result = perceptron(mixed, up_ref[layer], down_in[...])
        out_in[rows] = result.reshape(count, frames, own, width)
        store = pltpu.make_async_copy(out_in.at[rows], out_ref.at[rows], sems.at[2 + place])
        store.start()
        stores.append(store)
    for store in stores:
        store.wait()


def last_stage(layer, first, second, halo, weights, up, down):
    owners, frames, own, _ = first.shape
    return pl.pallas_call(
        functools.partial(last_kernel, layer),
        name="last_stage",
        out_shape=pltpu.HBM(first.shape, jnp.bfloat16),
        in_specs=vmem_specs(4) + hbm_specs(2),
        out_specs=hbm_specs(1)[0],
        scratch_shapes=[
            pltpu.VMEM(first.shape, jnp.bfloat16),
            pltpu.VMEM(first.shape, jnp.bfloat16),
            pltpu.VMEM(down.shape[1:], jnp.bfloat16),
            band_scratch(weights),
            pltpu.VMEM(first.shape, jnp.float32),
            pltpu.SemaphoreType.DMA((3 + owners * frames * own // ROWS,)),
        ],
        compiler_params=params(16 + 8 * first.size // MIB),
    )(*map(held, (second, halo, weights, up)), *map(in_hbm, (down, first)))


def direct(blocks):
    return lax.all_to_all(blocks, "snap", split_axis=0, concat_axis=0, tiled=True)


def runs_of(count):
    inner = count // OUTER
    inside = [list(range(first, first + inner)) for first in range(0, count, inner)]
    across = [list(range(first, count, inner)) for first in range(inner)]
    return inside, across


def inside_runs(blocks):
    count = blocks.shape[0]
    parted = blocks.reshape(OUTER, count // OUTER, *blocks.shape[1:])
    parted = lax.all_to_all(
        parted,
        "snap",
        split_axis=1,
        concat_axis=1,
        tiled=True,
        axis_index_groups=runs_of(count)[0],
    )
    return parted.reshape(blocks.shape)


def across_runs(blocks):
    count = blocks.shape[0]
    parted = blocks.reshape(OUTER, count // OUTER, *blocks.shape[1:])
    parted = lax.all_to_all(
        parted,
        "snap",
        split_axis=0,
        concat_axis=0,
        tiled=True,
        axis_index_groups=runs_of(count)[1],
    )
    return parted.reshape(blocks.shape)


def exchange_in_turn(blocks, second_begins, second_ends):
    span = lax.axis_index("span")
    late = BAND // blocks.shape[1]
    first = lax.cond(span == 0, direct, second_begins, blocks)
    halo = lax.ppermute(first[-late:], "span", [(0, 1)])
    blocks, begun = lax.optimization_barrier((blocks, first))
    second = lax.cond(
        span == 0,
        lambda blocks, begun: blocks,
        lambda blocks, begun: second_ends(blocks, begun),
        blocks,
        begun,
    )
    return first, second, halo


def local(
    features,
    block_values,
    block_cols,
    block_counts,
    band_coeffs,
    graph_layer_weight,
    up_weight,
    down_weight,
):
    snaps = lax.axis_size("snap")
    frames, vertices, width = features.shape[1:]
    sent, dense, weights = first_graph(
        features,
        graph_layer_weight,
        block_values,
        block_cols,
        block_counts,
        band_coeffs,
        snaps,
    )
    for layer in range(LAYERS - 1):
        arrived = exchange_in_turn(sent, inside_runs, lambda blocks, begun: across_runs(begun))
        rows = direct(middle_stage(layer, *arrived, weights, up_weight, down_weight))
        sent, spare = later_graph(layer, rows, up_weight, down_weight, graph_layer_weight, dense)
    arrived = exchange_in_turn(
        sent, lambda blocks: spare, lambda blocks, begun: direct(blocks)
    )
    out = last_stage(LAYERS - 1, *arrived, weights, up_weight, down_weight)
    return out.reshape(1, snaps * frames, vertices // snaps, width)


def solution(mesh):
    in_specs = (
        P("span", "snap", None, None),
        P("span", "snap", None, None, None, None),
        P("span", "snap", None, None),
        P("span", "snap", None),
        P("span", None, None),
        P(),
        P(),
        P(),
    )
    out_specs = P("span", None, "snap", None)
    return jax.shard_map(local, mesh=mesh, in_specs=in_specs, out_specs=out_specs, check_vma=False)
```

```python
import functools

import jax
import jax.numpy as jnp
from jax import lax
from jax.experimental import pallas as pl
from jax.experimental.pallas import tpu as pltpu
from jax.sharding import PartitionSpec as P

BAND = 32
LAYERS = 2
TILE = 256
REACH = 3
ROWS = 512
GROUP = 16
OUTER = 4
MIB = 1 << 20


def dot(left, right):
    return jnp.dot(left, right, preferred_element_type=jnp.float32)


def in_vmem(shape, dtype=jnp.bfloat16):
    return pltpu.VMEM(shape, dtype)


def vmem_specs(count):
    return [pl.BlockSpec(memory_space=pltpu.VMEM)] * count


def held(array):
    return pltpu.with_memory_space_constraint(array, pltpu.VMEM)


def in_hbm(array):
    return pltpu.with_memory_space_constraint(array, pltpu.HBM)


def hbm_specs(count):
    return [pl.BlockSpec(memory_space=pltpu.HBM)] * count


def params(mib=16):
    return pltpu.CompilerParams(vmem_limit_bytes=mib * MIB)


def copies(pairs, sems):
    return [pltpu.make_async_copy(*pair, sems.at[place]) for place, pair in enumerate(pairs)]


def lay_out(frame, values_ref, cols_ref, counts_ref, dense_ref):
    block_rows, slots, size, _ = values_ref.shape[1:]
    dense_ref[frame] = jnp.zeros(dense_ref.shape[1:], dense_ref.dtype)
    for row in range(block_rows):
        for slot in reversed(range(slots)):
            column = pl.multiple_of(cols_ref[frame, row, slot] * size, size)
            block = values_ref[frame, row, slot]
            used = slot < counts_ref[frame, row]
            dense_ref[frame, pl.ds(row * size, size), pl.ds(column, size)] = jnp.where(
                used, block, jnp.zeros_like(block)
            )


def propagate(frame, dense_ref, weighted, sent_ref):
    vertices = dense_ref.shape[1]
    rows = min(vertices, 512)
    own, width = sent_ref.shape[2:]
    for first in range(0, vertices, rows):
        summed = dot(dense_ref[frame, pl.ds(first, rows)], weighted).astype(jnp.bfloat16)
        sent_ref[pl.ds(first // own, rows // own), frame] = summed.reshape(
            rows // own, own, width
        )


def band_rows(coeffs, first_frame, frames_in_tile, copies_of):
    frames = coeffs.shape[0]
    back = (REACH - 1) * frames_in_tile
    lags = lax.broadcasted_iota(jnp.int32, coeffs.shape, 1)
    here = first_frame + lax.broadcasted_iota(jnp.int32, coeffs.shape, 0)
    scaled = jnp.where(here >= lags, coeffs.astype(jnp.float32), 0.0)
    weights = scaled / jnp.sum(scaled, axis=1, keepdims=True)
    sources = REACH * frames_in_tile
    place = lax.broadcasted_iota(jnp.int32, (frames, sources), 0) % frames_in_tile
    lag = back + place - lax.broadcasted_iota(jnp.int32, (frames, sources), 1)
    chosen = jnp.zeros((frames, sources), jnp.float32)
    for each in range(BAND):
        chosen = jnp.where(lag == each, weights[:, each : each + 1], chosen)
    wide = sources * copies_of
    spread = (
        lax.broadcasted_iota(jnp.int32, (sources, wide), 1) // copies_of
        == lax.broadcasted_iota(jnp.int32, (sources, wide), 0)
    ).astype(jnp.bfloat16)
    return dot(chosen.astype(jnp.bfloat16), spread)


def first_kernel(
    features_ref,
    weight_ref,
    values_ref,
    cols_ref,
    counts_ref,
    coeffs_ref,
    sent_ref,
    dense_ref,
    band_ref,
    features_in,
    weight_in,
    values_in,
    cols_in,
    counts_in,
    coeffs_in,
    dense_in,
    sems,
):
    frames, vertices, width = features_in.shape
    loads = copies(
        [
            (coeffs_ref.at[0], coeffs_in),
            (weight_ref.at[0], weight_in),
            (features_ref.at[0, 0], features_in.at[0]),
            (cols_ref.at[0], cols_in),
            (counts_ref.at[0], counts_in),
            (values_ref.at[0], values_in),
            *((features_ref.at[0, frame], features_in.at[frame]) for frame in range(1, frames)),
        ],
        sems,
    )
    for load in loads:
        load.start()
    loads[0].wait()
    first_frame = lax.axis_index("span") * coeffs_in.shape[0]
    band_ref[...] = band_rows(coeffs_in[...], first_frame, TILE // GROUP, GROUP)
    for load in loads[1:3]:
        load.wait()
    weighted = [dot(features_in[0], weight_in[...]).astype(jnp.bfloat16)]
    for load in loads[3:]:
        load.wait()
    for frame in range(frames):
        lay_out(frame, values_in, cols_in, counts_in, dense_in)
    for frame in range(1, frames):
        weighted.append(dot(features_in[frame], weight_in[...]).astype(jnp.bfloat16))
    store = pltpu.make_async_copy(dense_in, dense_ref, sems.at[len(loads)])
    store.start()
    for frame in range(frames):
        propagate(frame, dense_in, weighted[frame], sent_ref)
    store.wait()


def normed(mixed):
    mean_square = jnp.mean(mixed * mixed, axis=-1, keepdims=True)
    return (mixed * lax.rsqrt(mean_square + 1e-06)).astype(jnp.bfloat16)


def perceptron(mixed, up, down):
    active = jnp.maximum(dot(normed(mixed), up), 0.0).astype(jnp.bfloat16)
    return (mixed + dot(active, down)).astype(jnp.bfloat16)


def later_kernel(
    layer, arrived_ref, up_ref, down_ref, next_ref, dense_ref, sent_ref, spare_ref, rows_ref
):
    _, frames, own, width = arrived_ref.shape
    vertices = dense_ref.shape[1]
    batch = ROWS // (frames * own)
    span = lax.axis_index("span")

    @pl.when(span == 0)
    def work():
        for first in range(0, arrived_ref.shape[0], batch):
            mixed = arrived_ref[pl.ds(first, batch)].reshape(ROWS, width)
            done = perceptron(mixed.astype(jnp.float32), up_ref[layer], down_ref[layer])
            done = done.reshape(batch, frames, own, width)
            for frame in range(frames):
                rows_ref[frame, pl.ds(first * own, batch * own)] = done[:, frame].reshape(
                    batch * own, width
                )

    @pl.when(span == 1)
    def gather():
        for frame in range(frames):
            rows_ref[frame] = arrived_ref[:, frame].reshape(vertices, width)

    weighted = dot(rows_ref[...].reshape(frames * vertices, width), next_ref[layer + 1])
    weighted = weighted.astype(jnp.bfloat16).reshape(frames, vertices, width)
    for frame in range(frames):
        propagate(frame, dense_ref, weighted[frame], sent_ref)


def first_graph(features, weight, values, cols, counts, coeffs, owners):
    frames, vertices, width = features.shape[1:]
    own = vertices // owners
    large = 2 * (features.size + values.size + frames * vertices * vertices)
    return pl.pallas_call(
        first_kernel,
        name="first_graph",
        out_shape=[
            in_vmem((owners, frames, own, width)),
            pltpu.HBM((frames, vertices, vertices), jnp.bfloat16),
            in_vmem((coeffs.shape[1], REACH * TILE), jnp.float32),
        ],
        in_specs=hbm_specs(6),
        out_specs=vmem_specs(1) + hbm_specs(1) + vmem_specs(1),
        scratch_shapes=[
            pltpu.VMEM(features.shape[1:], jnp.bfloat16),
            pltpu.VMEM(weight.shape[1:], jnp.bfloat16),
            pltpu.VMEM(values.shape[1:], jnp.bfloat16),
            pltpu.SMEM(cols.shape[1:], jnp.int32),
            pltpu.SMEM(counts.shape[1:], jnp.int32),
            pltpu.VMEM(coeffs.shape[1:], jnp.int32),
            pltpu.VMEM((frames, vertices, vertices), jnp.bfloat16),
            pltpu.SemaphoreType.DMA((6 + frames,)),
        ],
        compiler_params=params(17 + large // MIB),
    )(*map(in_hbm, (features, weight, values, cols, counts, coeffs)))


def later_graph(layer, mixed, up, down, following, dense):
    _, frames, _, width = mixed.shape
    return pl.pallas_call(
        functools.partial(later_kernel, layer),
        name="later_graph",
        out_shape=[in_vmem(mixed.shape), pltpu.HBM(mixed.shape, jnp.bfloat16)],
        in_specs=vmem_specs(5),
        out_specs=vmem_specs(1) + hbm_specs(1),
        scratch_shapes=[pltpu.VMEM((frames, dense.shape[1], width), jnp.bfloat16)],
        compiler_params=params(),
    )(*map(held, (mixed, up, down, following, dense)))


def band_tile(rows):
    frames, wide = rows.shape
    full = jnp.broadcast_to(rows[:, None, :], (frames, GROUP, wide)).reshape(
        frames * GROUP, wide
    )
    same = (
        lax.broadcasted_iota(jnp.int32, full.shape, 0) % GROUP
        == lax.broadcasted_iota(jnp.int32, full.shape, 1) % GROUP
    )
    return jnp.where(same, full, 0.0).astype(jnp.bfloat16)


def spread(weights_ref, band_ref):
    in_tile = TILE // GROUP
    for tile in range(band_ref.shape[0]):
        full = band_tile(weights_ref[pl.ds(tile * in_tile, in_tile)])
        for source in range(REACH):
            band_ref[tile, source] = full[:, source * TILE : (source + 1) * TILE]


def tile_index(ref, tile, group):
    steps = TILE // (GROUP * ref.shape[1])
    return (pl.ds(tile * steps, steps), slice(None), pl.ds(group * GROUP, GROUP))


def mix(tile, group, arrived_ref, halo_ref, band_ref):
    before = REACH - 1
    total = None
    for part in range(REACH):
        source = tile + part - before
        if source < 0 and halo_ref is None:
            continue
        ref, source = (arrived_ref, source) if source >= 0 else (halo_ref, source + before)
        rows = ref[tile_index(ref, source, group)].reshape(TILE, ref.shape[3])
        term = dot(band_ref[tile, part], rows)
        total = term if total is None else total + term
    return total


def put(tile, group, rows, ref):
    index = tile_index(ref, tile, group)
    ref[index] = rows.reshape(index[0].size, ref.shape[1], GROUP, -1)


def keep_first(first_ref, arrived_ref):
    @pl.when(lax.axis_index("span") == 0)
    def keep():
        arrived_ref[...] = first_ref[...]


def band_scratch(weights):
    return pltpu.VMEM((weights.shape[0] * GROUP // TILE, REACH, TILE, TILE), jnp.bfloat16)


def middle_kernel(
    layer,
    first_ref,
    halo_ref,
    weights_ref,
    second_ref,
    up_ref,
    down_ref,
    sent_ref,
    arrived_ref,
    up_in,
    down_in,
    band_ref,
    mixed_ref,
    sems,
):
    second_core = lax.axis_index("span") == 1
    loads = copies(
        [
            (second_ref, arrived_ref),
            (up_ref.at[layer], up_in),
            (down_ref.at[layer], down_in),
        ],
        sems,
    )

    @pl.when(second_core)
    def load_own():
        for load in loads:
            load.start()

    spread(weights_ref, band_ref)
    keep_first(first_ref, arrived_ref)

    @pl.when(second_core)
    def wait_own():
        loads[0].wait()

    owners, frames, own, width = arrived_ref.shape

    def mix_all(earlier_ref):
        for group in range(own // GROUP):
            for tile in range(band_ref.shape[0]):
                mixed = mix(tile, group, arrived_ref, earlier_ref, band_ref)
                put(tile, group, mixed, mixed_ref)

    @pl.when(second_core)
    def mix_second():
        mix_all(halo_ref)

    @pl.when(jnp.logical_not(second_core))
    def mix_first():
        mix_all(None)

    @pl.when(second_core)
    def work():
        for load in loads[1:]:
            load.wait()
        batch = ROWS // (frames * own)
        for first in range(0, owners, batch):
            rows = pl.ds(first, batch)
            result = perceptron(mixed_ref[rows].reshape(ROWS, width), up_in[...], down_in[...])
            sent_ref[rows] = result.reshape(batch, frames, own, width)

    @pl.when(jnp.logical_not(second_core))
    def leave():
        sent_ref[...] = mixed_ref[...].astype(jnp.bfloat16)


def middle_stage(layer, first, second, halo, weights, up, down):
    return pl.pallas_call(
        functools.partial(middle_kernel, layer),
        name="middle_stage",
        out_shape=in_vmem(first.shape),
        in_specs=vmem_specs(3) + hbm_specs(3),
        out_specs=vmem_specs(1)[0],
        scratch_shapes=[
            pltpu.VMEM(first.shape, jnp.bfloat16),
            pltpu.VMEM(up.shape[1:], jnp.bfloat16),
            pltpu.VMEM(down.shape[1:], jnp.bfloat16),
            band_scratch(weights),
            pltpu.VMEM(first.shape, jnp.float32),
            pltpu.SemaphoreType.DMA((3,)),
        ],
        compiler_params=params(16 + 6 * first.size // MIB),
    )(*map(held, (first, halo, weights)), *map(in_hbm, (second, up, down)))


def last_kernel(
    layer,
    second_ref,
    halo_ref,
    weights_ref,
    up_ref,
    down_ref,
    first_ref,
    out_ref,
    arrived_ref,
    out_in,
    down_in,
    band_ref,
    mixed_ref,
    sems,
):
    load = pltpu.make_async_copy(down_ref.at[layer], down_in, sems.at[0])
    load.start()
    span = lax.axis_index("span")

    @pl.when(span == 0)
    def fetch():
        own = pltpu.make_async_copy(first_ref, arrived_ref, sems.at[1])
        own.start()
        own.wait()

    @pl.when(span == 1)
    def keep():
        arrived_ref[...] = second_ref[...]

    spread(weights_ref, band_ref)
    owners, frames, own, width = arrived_ref.shape
    for group in range(own // GROUP):
        for tile in range(band_ref.shape[0]):
            put(tile, group, mix(tile, group, arrived_ref, halo_ref, band_ref), mixed_ref)
    load.wait()
    batch = ROWS // (frames * own)
    parts = [(first, batch) for first in range(0, owners - batch, batch)]
    parts += [(owners - batch, batch // 2), (owners - batch // 2, batch // 2)]
    stores = []
    for place, (first, count) in enumerate(parts):
        rows = pl.ds(first, count)
        mixed = mixed_ref[rows].reshape(count * frames * own, width)
        result = perceptron(mixed, up_ref[layer], down_in[...])
        out_in[rows] = result.reshape(count, frames, own, width)
        store = pltpu.make_async_copy(out_in.at[rows], out_ref.at[rows], sems.at[2 + place])
        store.start()
        stores.append(store)
    for store in stores:
        store.wait()


def last_stage(layer, first, second, halo, weights, up, down):
    owners, frames, own, _ = first.shape
    return pl.pallas_call(
        functools.partial(last_kernel, layer),
        name="last_stage",
        out_shape=pltpu.HBM(first.shape, jnp.bfloat16),
        in_specs=vmem_specs(4) + hbm_specs(2),
        out_specs=hbm_specs(1)[0],
        scratch_shapes=[
            pltpu.VMEM(first.shape, jnp.bfloat16),
            pltpu.VMEM(first.shape, jnp.bfloat16),
            pltpu.VMEM(down.shape[1:], jnp.bfloat16),
            band_scratch(weights),
            pltpu.VMEM(first.shape, jnp.float32),
            pltpu.SemaphoreType.DMA((3 + owners * frames * own // ROWS,)),
        ],
        compiler_params=params(16 + 8 * first.size // MIB),
    )(*map(held, (second, halo, weights, up)), *map(in_hbm, (down, first)))


def direct(blocks):
    return lax.all_to_all(blocks, "snap", split_axis=0, concat_axis=0, tiled=True)


def runs_of(count):
    inner = count // OUTER
    inside = [list(range(first, first + inner)) for first in range(0, count, inner)]
    across = [list(range(first, count, inner)) for first in range(inner)]
    return inside, across


def inside_runs(blocks):
    count = blocks.shape[0]
    parted = blocks.reshape(OUTER, count // OUTER, *blocks.shape[1:])
    parted = lax.all_to_all(
        parted,
        "snap",
        split_axis=1,
        concat_axis=1,
        tiled=True,
        axis_index_groups=runs_of(count)[0],
    )
    return parted.reshape(blocks.shape)


def across_runs(blocks):
    count = blocks.shape[0]
    parted = blocks.reshape(OUTER, count // OUTER, *blocks.shape[1:])
    parted = lax.all_to_all(
        parted,
        "snap",
        split_axis=0,
        concat_axis=0,
        tiled=True,
        axis_index_groups=runs_of(count)[1],
    )
    return parted.reshape(blocks.shape)


def exchange_in_turn(blocks, second_begins, second_ends):
    span = lax.axis_index("span")
    late = BAND // blocks.shape[1]
    first = lax.cond(span == 0, direct, second_begins, blocks)
    halo = lax.ppermute(first[-late:], "span", [(0, 1)])
    blocks, begun = lax.optimization_barrier((blocks, first))
    second = lax.cond(
        span == 0,
        lambda blocks, begun: blocks,
        lambda blocks, begun: second_ends(blocks, begun),
        blocks,
        begun,
    )
    return first, second, halo


def local(
    features,
    block_values,
    block_cols,
    block_counts,
    band_coeffs,
    graph_layer_weight,
    up_weight,
    down_weight,
):
    snaps = lax.axis_size("snap")
    frames, vertices, width = features.shape[1:]
    sent, dense, weights = first_graph(
        features,
        graph_layer_weight,
        block_values,
        block_cols,
        block_counts,
        band_coeffs,
        snaps,
    )
    for layer in range(LAYERS - 1):
        arrived = exchange_in_turn(sent, inside_runs, lambda blocks, begun: across_runs(begun))
        rows = direct(middle_stage(layer, *arrived, weights, up_weight, down_weight))
        sent, spare = later_graph(layer, rows, up_weight, down_weight, graph_layer_weight, dense)
    arrived = exchange_in_turn(
        sent, lambda blocks: spare, lambda blocks, begun: direct(blocks)
    )
    out = last_stage(LAYERS - 1, *arrived, weights, up_weight, down_weight)
    return out.reshape(1, snaps * frames, vertices // snaps, width)


def solution(mesh):
    in_specs = (
        P("span", "snap", None, None),
        P("span", "snap", None, None, None, None),
        P("span", "snap", None, None),
        P("span", "snap", None),
        P("span", None, None),
        P(),
        P(),
        P(),
    )
    out_specs = P("span", None, "snap", None)
    return jax.shard_map(local, mesh=mesh, in_specs=in_specs, out_specs=out_specs, check_vma=False)
```
